512 devices in a mesh: row: 32 (over z, core), col: 16 (over x, y).
Axes of the slice: x: 4, y: 4, z: 16, core: 2. Of those that a mesh axis runs over, the one named last changes fastest.
Arguments:
- blocks: bfloat16 [16384, 128, 128], P(('row', 'col')), may hold values from -0.09375 to 0.09375
- block_rows: int32 [16384], P(('row', 'col')), may hold values from 0 to 512, as said below
- block_cols: int32 [16384], P(('row', 'col')), may hold values from 0 to 512, as said below
- start: float32 [64, 65536], P(None, ('row', 'col'))
Outputs:
- basis: float32 [64, 65536], P(None, ('row', 'col'))
- alphas: float32 [3, 64, 64], replicated
- betas: float32 [3, 64, 64], replicated
The draws below stay inside these ranges and needn't reach their ends.
Inputs may be any that keep to these rules, and one draw needn't show every extreme that they name: For device d the entries d * 32 to (d + 1) * 32 - 1 list its stored blocks first and then empty slots, which hold 512 in both lists. A stored block (i, j) has i <= j, i // 16 equal to the device's row index, j % 16 equal to its col index, and no position is stored twice. The devices of row index 0 fill all 32 slots; block_cols holds 512 exactly where block_rows does. `block_cols`: see block_rows.
All inputs are finite; a program needn't handle non-finite values.
Results may differ from the reference program's by a relative error of at most 0.04.
Values may be sent and summed in bfloat16 or wider, within the bound.
A program may use at most 64 MiB of HBM per device.

```python
import jax
import jax.numpy as jnp
from jax import lax

K = 64
B = 128
SLOTS = 32
ITERS = 3
NB = 512
NVEC = 65536
N_ROW = 32
N_COL = 16
DEVICES = 512


def slot_lists(key):
    positions = N_COL * N_ROW
    device = jnp.arange(DEVICES, dtype=jnp.int32)
    row_index = device // N_COL
    col_index = device % N_COL
    place = jnp.arange(positions, dtype=jnp.int32)
    local_row = place // N_ROW
    local_col = place % N_ROW
    block_i = row_index[:, None] * N_COL + local_row[None, :]
    block_j = local_col[None, :] * N_COL + col_index[:, None]
    valid = (block_i <= block_j).astype(jnp.int32)
    keys = jax.random.split(jax.random.fold_in(key, 5), DEVICES)
    shuffled = jax.vmap(lambda single: jax.random.permutation(single, positions))(keys).astype(jnp.int32)
    scores = valid * (positions + shuffled) + (1 - valid) * shuffled
    order = jnp.argsort(-scores, axis=1, stable=True).astype(jnp.int32)
    padding = max(SLOTS - positions, 0)
    order = jnp.concatenate([order, jnp.zeros((DEVICES, padding), jnp.int32)], axis=1)[:, :SLOTS]
    valid_count = jnp.sum(valid, axis=1)
    extra = jax.random.randint(jax.random.fold_in(key, 6), (DEVICES,), 0, max(SLOTS // 8, 1)).astype(jnp.int32)
    wanted = SLOTS * (N_ROW - row_index) // N_ROW + extra
    wanted = jnp.where(row_index == 0, SLOTS, wanted)
    live_count = jnp.minimum(jnp.minimum(wanted, valid_count), SLOTS)
    live = jnp.arange(SLOTS, dtype=jnp.int32)[None, :] < live_count[:, None]
    chosen_i = jnp.take_along_axis(block_i, order, axis=1)
    chosen_j = jnp.take_along_axis(block_j, order, axis=1)
    rows_out = jnp.where(live, chosen_i, NB).reshape(-1).astype(jnp.int32)
    cols_out = jnp.where(live, chosen_j, NB).reshape(-1).astype(jnp.int32)
    return (rows_out, cols_out)


def draw_block_rows(key, part):
    return slot_lists(key)[0]


def draw_block_cols(key, part):
    return slot_lists(key)[1]


def draw_start(key, part):
    key = jax.random.fold_in(key, 3)
    scale_key = jax.random.fold_in(key, 1)
    value_key = jax.random.fold_in(key, 2)
    scales = jnp.exp(jax.random.uniform(scale_key, (1, NVEC), jnp.float32) * jnp.log(10.0))
    values = jax.random.normal(value_key, (K, NVEC), jnp.float32)
    return values * scales


def block_levels(key, dims, cuts, least, largest):
    def one(dim, parts):
        heights = jax.random.uniform(jax.random.fold_in(jax.random.fold_in(key, 6), dim), (parts,), jnp.float32, least / len(cuts), largest / len(cuts))
        return jnp.repeat(jnp.exp(heights), dims[dim] // parts).reshape((-1,) + (1,) * (len(dims) - dim - 1))

    loudness = one(*cuts[0])
    for cut in cuts[1:]:
        loudness = loudness * one(*cut)
    return loudness


def bell_draw(stream_key, dims, deviation, bound, cuts=(), kind=jnp.bfloat16):
    array = deviation * jax.random.normal(stream_key, dims, jnp.float32)
    if cuts:
        array = array * block_levels(stream_key, dims, cuts, -0.22, 0.18)
    return jnp.clip(array, -bound, bound).astype(kind)


def setup_inputs(seed: int = 0) -> dict:
    key_of = jax.random.split(jax.random.key(seed), 5)
    return {
        "blocks": bell_draw(key_of[0], (DEVICES * SLOTS, B, B), (B * SLOTS) ** -0.5, 0.09375, ((0, 512),)),
        "block_rows": draw_block_rows(jax.random.fold_in(key_of[4], 71), 0),
        "block_cols": draw_block_cols(jax.random.fold_in(key_of[4], 71), 0),
        "start": draw_start(jax.random.fold_in(key_of[4], 71), 0),
    }


HIGH = lax.Precision.HIGHEST

def apply_operator(blocks, block_rows, block_cols, vectors):
    width = vectors.shape[0]
    rounded = lax.optimization_barrier(vectors.astype(jnp.bfloat16)).astype(jnp.float32)
    padded = jnp.concatenate([rounded.reshape(width, NB, B), jnp.zeros((width, 1, B), jnp.float32)], axis=1)
    per_block = blocks.reshape(DEVICES, SLOTS, B, B)
    rows_dev = block_rows.reshape(DEVICES, SLOTS)
    cols_dev = block_cols.reshape(DEVICES, SLOTS)

    def one_device(carry, item):
        row_acc, col_acc = carry
        stored, rows_here, cols_here, device = item
        row_index = device // N_COL
        col_index = device % N_COL
        matrix = stored.astype(jnp.float32)
        taken_cols = padded[:, cols_here]
        forward = jnp.einsum('ksb,sdb->ksd', taken_cols, matrix, precision=HIGH)
        hot_rows = ((rows_here - row_index * N_COL)[:, None] == jnp.arange(N_COL)[None, :]).astype(jnp.float32)
        row_part = jnp.einsum('ksd,sm->kmd', forward, hot_rows, precision=HIGH)
        row_part = lax.optimization_barrier(row_part.astype(jnp.bfloat16)).astype(jnp.float32)
        taken_rows = padded[:, rows_here]
        backward = jnp.einsum('ksb,sbd->ksd', taken_rows, matrix, precision=HIGH)
        hot_cols = ((cols_here // N_COL)[:, None] == jnp.arange(N_ROW)[None, :]).astype(jnp.float32)
        col_part = jnp.einsum('ksd,sm->kmd', backward, hot_cols, precision=HIGH)
        col_part = lax.optimization_barrier(col_part.astype(jnp.bfloat16)).astype(jnp.float32)
        row_acc = row_acc.at[row_index].add(row_part)
        col_acc = col_acc.at[col_index].add(col_part)
        return ((row_acc, col_acc), None)
    start_acc = (jnp.zeros((N_ROW, width, N_COL, B), jnp.float32), jnp.zeros((N_COL, width, N_ROW, B), jnp.float32))
    items = (per_block, rows_dev, cols_dev, jnp.arange(DEVICES, dtype=jnp.int32))
    (row_acc, col_acc), unused = lax.scan(one_device, start_acc, items)
    row_sum = row_acc.transpose(1, 0, 2, 3).reshape(width, NVEC)
    col_sum = col_acc.transpose(1, 2, 0, 3).reshape(width, NVEC)
    return row_sum + col_sum

def inner(left, right):
    return jnp.dot(left, right.T, precision=HIGH) / NVEC

def normalize(vectors):
    gramian = inner(vectors, vectors)
    factor_low = jnp.linalg.cholesky(gramian)
    identity = jnp.eye(vectors.shape[0], dtype=jnp.float32)
    inverse = jax.scipy.linalg.solve_triangular(factor_low, identity, lower=True)
    return (jnp.dot(inverse, vectors, precision=HIGH), factor_low)

def reference(blocks, block_rows, block_cols, start):
    basis, factor_low = normalize(start)
    previous = None
    alpha_list = []
    beta_list = []
    for step in range(ITERS):
        residue = apply_operator(blocks, block_rows, block_cols, basis)
        if previous is not None:
            residue = residue - jnp.dot(factor_low.T, previous, precision=HIGH)
        alpha = inner(basis, residue)
        residue = residue - jnp.dot(alpha.T, basis, precision=HIGH)
        following, factor_low = normalize(residue)
        alpha_list.append(alpha)
        beta_list.append(factor_low)
        previous = basis
        basis = following
    return (basis, jnp.stack(alpha_list), jnp.stack(beta_list))
```

```python
import jax
import jax.numpy as jnp
from jax import lax
from jax.experimental import pallas as pl
from jax.experimental.pallas import tpu as pltpu
from jax.sharding import PartitionSpec as P

ITERS = 3
HIGH = lax.Precision.HIGHEST
MESH = pl.DeviceIdType.MESH
F32 = jnp.float32
BF16 = jnp.bfloat16

NZ = 16
NC = 16
SLOTS = 32
FAR = (8, 7, 9, 6, 10, 5, 11, 4, 12, 3, 13, 2, 14, 1, 15)


def nt(a, b):
    return lax.dot_general(a, b, (((1,), (1,)), ((), ())), precision=HIGH, preferred_element_type=F32)


def nn(a, b):
    return lax.dot_general(a, b, (((1,), (0,)), ((), ())), precision=HIGH, preferred_element_type=F32)


def plan_part(target, source, valid, targets):
    count = target.shape[0]
    ids = jnp.arange(count, dtype=jnp.int32)
    key = jnp.where(valid, target, targets) * count + ids
    rank = jnp.sum((key[None, :] < key[:, None]).astype(jnp.int32), axis=1)
    place = rank[None, :] == ids[:, None]
    perm = jnp.sum(jnp.where(place, ids[None, :], 0), axis=1)
    sorted_target = jnp.sum(jnp.where(place, (key // count)[None, :], 0), axis=1)
    sorted_source = jnp.sum(jnp.where(place, jnp.where(valid, source, 0)[None, :], 0), axis=1)
    before = jnp.concatenate([jnp.full((1,), -1, jnp.int32), sorted_target[:-1]])
    keep = (before == sorted_target).astype(jnp.int32)
    span = jnp.arange(SLOTS, dtype=jnp.int32)
    upto = jnp.sum((key[None, :] < (span[:, None] + 1) * count).astype(jnp.int32), axis=1)
    some = jnp.sum((target[None, :] == span[:, None]) & valid[None, :], axis=1)
    last = jnp.where(some > 0, upto - 1, count)
    return [perm, keep, sorted_source, last]


def factor(m_ref):
    rows = lax.broadcasted_iota(jnp.int32, (64, 1), 0)

    def block(b, carry):
        mat, diag = carry
        live = rows < 64 - 8 * b
        for j in range(8):
            pivot = mat[j : j + 1, j : j + 1]
            below = live & (rows > j)
            scaled = jnp.where(below, mat[:, j : j + 1], 0.0) * (1.0 / pivot)
            diag = jnp.where(rows == j, pivot, diag)
            mat = mat - scaled * mat[j : j + 1, :]
        mat = pltpu.roll(mat, 120, 1)
        mat = jnp.concatenate([mat[8:], mat[:8]], axis=0)
        diag = jnp.concatenate([diag[8:], diag[:8]], axis=0)
        return mat, diag

    mat, diag = lax.fori_loop(0, 8, block, (m_ref[...], jnp.zeros((64, 1), F32)))
    mat = pltpu.roll(mat, 64, 1) * lax.rsqrt(diag)
    lanes = lax.broadcasted_iota(jnp.int32, (64, 128), 1)
    row = lax.broadcasted_iota(jnp.int32, (64, 128), 0)
    m_ref[...] = jnp.where((lanes >= 64) | (lanes >= row), mat, 0.0)


def kernel(
    plan, start_ref, blocks_ref, basis_ref, alpha_ref, beta_ref,
    q_ref, y_ref, r_ref, x_ref, m_ref, sums,
    ag_src, stripe_0, stripe_1, stripe_2, colset_0, colset_1, colset_2, pair_src, pair_dst, zed_src, zed_dst, row_src, row_dst,
    ar_src, ar1, ar_s1, ar2, ar_s2, ar3, ar_s3, ar4,
    op_send, op_recv, ar_send, ar_recv,
):
    r = lax.axis_index("row")
    c = lax.axis_index("col")
    z, k = r // 2, lax.rem(r, 2)
    cp, ch = lax.rem(c, 8), c // 8
    sibling = (z * 2 + (1 - k), c)

    def along_z(o):
        there = lax.rem(z + o, NZ)
        return there, (there * 2 + k, c)

    def along_c(o):
        there = lax.rem(c + o, NC)
        return there, (r, there)

    barrier = pltpu.get_barrier_semaphore()
    for o in range(1, 16):
        pl.semaphore_signal(barrier, inc=1, device_id=along_z(o)[1], device_id_type=MESH)
        pl.semaphore_signal(barrier, inc=1, device_id=along_c(o)[1], device_id_type=MESH)
    pl.semaphore_signal(barrier, inc=1, device_id=sibling, device_id_type=MESH)
    pl.semaphore_wait(barrier, 31)

    stripes = (stripe_0, stripe_1, stripe_2)
    colsets = (colset_0, colset_1, colset_2)

    def push(src, dst, send, recv, where):
        pltpu.make_async_remote_copy(
            src_ref=src, dst_ref=dst, send_sem=send, recv_sem=recv, device_id=where, device_id_type=MESH
        ).start()

    def settle(ref, sem):
        pltpu.make_async_copy(ref, ref, sem).wait()

    sums[SLOTS] = jnp.zeros((64, 128), F32)

    def reduce_1(s):
        ar_src[s] = x_ref[...].reshape(8, 8, 128)
        ar1[s, c] = ar_src[s, cp]
        for o in range(1, 16):
            there, where = along_c(o)
            push(ar_src.at[s, lax.rem(there, 8)], ar1.at[s, c], ar_send.at[s, 0], ar_recv.at[s, 0], where)

    def reduce_2(s):
        settle(ar1.at[s, pl.ds(0, 15)], ar_recv.at[s, 0])
        total = ar1[s, 0]
        for i in range(1, 16):
            total = total + ar1[s, i]
        ar_s1[s] = total
        push(ar_s1.at[s], ar2.at[s], ar_send.at[s, 1], ar_recv.at[s, 1], sibling)
        settle(ar2.at[s], ar_recv.at[s, 1])
        ar_s2[s] = ar_s1[s] + ar2[s]
        ar3[s, z] = ar_s2[s]
        for o in FAR:
            push(ar_s2.at[s], ar3.at[s, z], ar_send.at[s, 2], ar_recv.at[s, 2], along_z(o)[1])

    def reduce_3(s):
        settle(ar3.at[s, pl.ds(0, 15)], ar_recv.at[s, 2])
        total = ar3[s, 0]
        for i in range(1, 16):
            total = total + ar3[s, i]
        ar_s3[s] = total
        ar4[s, cp] = total
        for o in range(1, 8):
            there = ch * 8 + lax.rem(cp + o, 8)
            push(ar_s3.at[s], ar4.at[s, cp], ar_send.at[s, 3], ar_recv.at[s, 3], (r, there))

    def reduce_4(s):
        settle(ar4.at[s, pl.ds(0, 7)], ar_recv.at[s, 3])
        x_ref[...] = ar4[s].reshape(64, 128) * (1.0 / (512 * 128))

    def reduce_end(s):
        settle(ar1.at[s, pl.ds(0, 15)], ar_send.at[s, 0])
        settle(ar2.at[s], ar_send.at[s, 1])
        settle(ar3.at[s, pl.ds(0, 15)], ar_send.at[s, 2])
        settle(ar4.at[s, pl.ds(0, 7)], ar_send.at[s, 3])

    def spread(t, value):
        ag_src[t] = value.astype(BF16)
        stripes[t][c] = ag_src[t]
        colsets[t][k * 16 + z] = ag_src[t]
        row_dst[t, c] = jnp.zeros((64, 128), BF16)
        zed_dst[t, z] = jnp.zeros((64, 128), BF16)
        for o, p in zip(FAR, range(1, 16)):
            push(ag_src.at[t], colsets[t].at[k * 16 + z], op_send.at[t, 0], op_recv.at[t, 0], along_z(o)[1])
            push(ag_src.at[t], stripes[t].at[c], op_send.at[t, 1], op_recv.at[t, 1], along_c(p)[1])

    def products(base, source, transposed):
        dims = (((1,), (1,)), ((), ())) if transposed else (((1,), (0,)), ((), ()))

        def one(p, total):
            part = lax.dot_general(
                source[plan[base + 64 + p]], blocks_ref[plan[base + p]], dims, preferred_element_type=F32
            )
            total = jnp.where(plan[base + 32 + p] > 0, total, 0.0) + part
            sums[p] = total
            return total

        lax.fori_loop(0, SLOTS, one, jnp.zeros((64, 128), F32), unroll=8)

    def backward(t):
        settle(stripes[t].at[pl.ds(0, 15)], op_recv.at[t, 1])
        products(128, stripes[t], False)
        for i in range(NZ):
            pair_src[t, i] = sums[plan[224 + (1 - k) * 16 + i]].astype(BF16)
        push(pair_src.at[t], pair_dst.at[t], op_send.at[t, 2], op_recv.at[t, 2], sibling)
        settle(pair_dst.at[t], op_recv.at[t, 2])
        for o in FAR:
            there, where = along_z(o)
            zed_src[t, there] = (sums[plan[224 + k * 16 + there]] + pair_dst[t, there].astype(F32)).astype(BF16)
            push(zed_src.at[t, there], zed_dst.at[t, z], op_send.at[t, 3], op_recv.at[t, 3], where)
        return sums[plan[224 + k * 16 + z]] + pair_dst[t, z].astype(F32)

    def relay(t):
        settle(colsets[t].at[pl.ds(0, 15)], op_recv.at[t, 0])
        half = pl.ds(k * 16, 16)
        push(colsets[t].at[half], colsets[t].at[half], op_send.at[t, 4], op_recv.at[t, 4], sibling)
        settle(colsets[t].at[pl.ds(0, 16)], op_recv.at[t, 4])

    def forward(t):
        products(0, colsets[t], True)
        for o in range(1, 16):
            there, where = along_c(o)
            row_src[t, there] = sums[plan[96 + there]].astype(BF16)
            push(row_src.at[t, there], row_dst.at[t, c], op_send.at[t, 5], op_recv.at[t, 5], where)
        return sums[plan[96 + c]]

    def collect(t, own):
        settle(row_dst.at[t, pl.ds(0, 15)], op_recv.at[t, 5])
        total = own
        for i in range(NC):
            total = total + row_dst[t, i].astype(F32)
        settle(zed_dst.at[t, pl.ds(0, 15)], op_recv.at[t, 3])
        for i in range(NZ):
            total = total + zed_dst[t, i].astype(F32)
        return total

    def operator_end(t):
        settle(colsets[t].at[pl.ds(0, 15)], op_send.at[t, 0])
        settle(stripes[t].at[pl.ds(0, 15)], op_send.at[t, 1])
        settle(pair_dst.at[t], op_send.at[t, 2])
        settle(zed_dst.at[t, pl.ds(0, 15)], op_send.at[t, 3])
        settle(colsets[t].at[pl.ds(0, 16)], op_send.at[t, 4])
        settle(row_dst.at[t, pl.ds(0, 15)], op_send.at[t, 5])

    lanes = lax.broadcasted_iota(jnp.int32, (64, 64), 1)
    rows = lax.broadcasted_iota(jnp.int32, (64, 64), 0)
    eye = (lanes == rows).astype(F32)

    def factor_start():
        m_ref[:, 0:64] = x_ref[:, 0:64]
        m_ref[:, 64:128] = eye
        factor(m_ref)

    def factor_step(t):
        alpha_t = x_ref[:, 64:128]
        alpha_ref[t] = alpha_t
        m_ref[:, 0:64] = x_ref[:, 0:64] - nt(alpha_t, alpha_t)
        m_ref[:, 64:128] = eye
        factor(m_ref)
        beta_ref[t] = m_ref[:, 0:64]
        return alpha_t

    first = start_ref[...]
    x_ref[...] = nt(first, jnp.concatenate([first, first], axis=0))
    reduce_1(0)
    reduce_2(0)
    reduce_3(0)
    reduce_4(0)
    factor_start()
    q_ref[...] = nn(m_ref[:, 64:128], first)
    spread(0, q_ref[...])
    own = backward(0)
    relay(0)
    own = own + forward(0)
    reduce_end(0)
    y_ref[...] = collect(0, own)
    r_ref[...] = y_ref[...]
    operator_end(0)

    def gram(s):
        x_ref[...] = nt(r_ref[...], jnp.concatenate([r_ref[...], q_ref[...]], axis=0))
        reduce_1(s)

    def step(s):
        spread(s, r_ref[...])
        gram(s)
        own = backward(s)
        reduce_2(s)
        relay(s)
        own = own + forward(s)
        reduce_3(s)
        reduce_4(s)
        alpha_t = factor_step(s - 1)
        inverse = m_ref[:, 64:128]
        following = nn(inverse, r_ref[...] - nn(alpha_t, q_ref[...]))
        reduce_end(s)
        image = collect(s, own)
        y_ref[...] = nn(inverse, image - nn(alpha_t, y_ref[...]))
        r_ref[...] = y_ref[...] - nn(m_ref[:, 0:64], q_ref[...])
        q_ref[...] = following
        operator_end(s)

    for s in range(1, ITERS):
        step(s)
    gram(ITERS)
    reduce_2(ITERS)
    reduce_3(ITERS)
    reduce_4(ITERS)
    alpha_t = factor_step(ITERS - 1)
    basis_ref[...] = nn(m_ref[:, 64:128], r_ref[...] - nn(alpha_t, q_ref[...]))
    reduce_end(ITERS)


def shards(blocks, block_rows, block_cols, start):
    row_index = lax.axis_index("row")
    valid = block_rows < 512
    row_target = block_rows - row_index * NC
    col_owner = block_cols // NC
    col_target = lax.rem(col_owner, 2) * NZ + col_owner // 2
    plan = jnp.concatenate(
        plan_part(row_target, col_target, valid, NC) + plan_part(col_target, row_target, valid, 2 * NZ)
    )
    vmem = pl.BlockSpec(memory_space=pltpu.VMEM)
    wide = (ITERS, 16, 64, 128)
    tall = (ITERS + 1, 16, 8, 128)
    piece = (ITERS + 1, 8, 128)
    basis, alphas, betas = pl.pallas_call(
        kernel,
        out_shape=(
            jax.ShapeDtypeStruct((64, 128), F32),
            jax.ShapeDtypeStruct((ITERS, 64, 64), F32),
            jax.ShapeDtypeStruct((ITERS, 64, 64), F32),
        ),
        in_specs=[pl.BlockSpec(memory_space=pltpu.SMEM), vmem, vmem],
        out_specs=(vmem, vmem, vmem),
        scratch_shapes=[
            pltpu.VMEM((64, 128), F32),
            pltpu.VMEM((64, 128), F32),
            pltpu.VMEM((64, 128), F32),
            pltpu.VMEM((64, 128), F32),
            pltpu.VMEM((64, 128), F32),
            pltpu.VMEM((SLOTS + 1, 64, 128), F32),
            pltpu.VMEM((ITERS, 64, 128), BF16),
            pltpu.VMEM(wide[1:], BF16),
            pltpu.VMEM(wide[1:], BF16),
            pltpu.VMEM(wide[1:], BF16),
            pltpu.VMEM((32, 64, 128), BF16),
            pltpu.VMEM((32, 64, 128), BF16),
            pltpu.VMEM((32, 64, 128), BF16),
            pltpu.VMEM(wide, BF16),
            pltpu.VMEM(wide, BF16),
            pltpu.VMEM(wide, BF16),
            pltpu.VMEM(wide, BF16),
            pltpu.VMEM(wide, BF16),
            pltpu.VMEM(wide, BF16),
            pltpu.VMEM((ITERS + 1, 8, 8, 128), F32),
            pltpu.VMEM(tall, F32),
            pltpu.VMEM(piece, F32),
            pltpu.VMEM(piece, F32),
            pltpu.VMEM(piece, F32),
            pltpu.VMEM(tall, F32),
            pltpu.VMEM(piece, F32),
            pltpu.VMEM((ITERS + 1, 8, 8, 128), F32),
            pltpu.SemaphoreType.DMA((ITERS, 6)),
            pltpu.SemaphoreType.DMA((ITERS, 6)),
            pltpu.SemaphoreType.DMA((ITERS + 1, 4)),
            pltpu.SemaphoreType.DMA((ITERS + 1, 4)),
        ],
        compiler_params=pltpu.CompilerParams(collective_id=0, has_side_effects=True, vmem_limit_bytes=36 << 20),
        name="lanczos",
    )(plan, start, blocks)
    return (basis, jnp.swapaxes(alphas, 1, 2), jnp.swapaxes(betas, 1, 2))


def solution(mesh):
    in_specs = (
        P(("row", "col"), None, None),
        P(("row", "col")),
        P(("row", "col")),
        P(None, ("row", "col")),
    )
    out_specs = (P(None, ("row", "col")), P(), P())
    return jax.shard_map(shards, mesh=mesh, in_specs=in_specs, out_specs=out_specs, check_vma=False)
```

```python
import jax
import jax.numpy as jnp
from jax import lax
from jax.experimental import pallas as pl
from jax.experimental.pallas import tpu as pltpu
from jax.sharding import PartitionSpec as P

ITERS = 3
HIGH = lax.Precision.HIGHEST
MESH = pl.DeviceIdType.MESH
F32 = jnp.float32
BF16 = jnp.bfloat16

NZ = 16
NC = 16
SLOTS = 32
REACH = (0, 3, 13, 6, 10, 8, 15, 2, 12, 5, 9, 1, 4, 14, 7, 11)
FAR = (8, 7, 9, 6, 10, 5, 11, 4, 12, 3, 13, 2, 14, 1, 15)


def nt(a, b):
    return lax.dot_general(a, b, (((1,), (1,)), ((), ())), precision=HIGH, preferred_element_type=F32)


def nn(a, b):
    return lax.dot_general(a, b, (((1,), (0,)), ((), ())), precision=HIGH, preferred_element_type=F32)


def plan_part(target, source, valid, targets):
    count = target.shape[0]
    ids = jnp.arange(count, dtype=jnp.int32)
    key = jnp.where(valid, target, targets) * count + ids
    rank = jnp.sum((key[None, :] < key[:, None]).astype(jnp.int32), axis=1)
    place = rank[None, :] == ids[:, None]
    perm = jnp.sum(jnp.where(place, ids[None, :], 0), axis=1)
    sorted_target = jnp.sum(jnp.where(place, (key // count)[None, :], 0), axis=1)
    sorted_source = jnp.sum(jnp.where(place, jnp.where(valid, source, 0)[None, :], 0), axis=1)
    before = jnp.concatenate([jnp.full((1,), -1, jnp.int32), sorted_target[:-1]])
    keep = (before == sorted_target).astype(jnp.int32)
    span = jnp.arange(SLOTS, dtype=jnp.int32)
    upto = jnp.sum((key[None, :] < (span[:, None] + 1) * count).astype(jnp.int32), axis=1)
    some = jnp.sum((target[None, :] == span[:, None]) & valid[None, :], axis=1)
    last = jnp.where(some > 0, upto - 1, count)
    return [perm, keep, sorted_source, last]


def factor(m_ref):
    rest = m_ref[...]
    done = []
    for b in range(8):
        shape = rest.shape
        row = lax.broadcasted_iota(jnp.int32, shape, 0)
        cols = [jnp.broadcast_to(rest[:, 8 * b + i : 8 * b + i + 1], shape) for i in range(8)]
        for j in range(0, 8, 2):
            c0, c1 = cols[j], cols[j + 1]
            one, off, two = c0[j : j + 1], c0[j + 1 : j + 2], c1[j + 1 : j + 2]
            inv0 = 1.0 / one
            inv1 = one * (1.0 / (one * two - off * off))
            share = off * inv0
            r0 = rest[j : j + 1]
            r1 = rest[j + 1 : j + 2] - share * r0
            c1 = c1 - share * c0
            for i in range(j + 2, 8):
                cols[i] = cols[i] - c0 * (c0[i : i + 1] * inv0) - c1 * (c1[i : i + 1] * inv1)
            low = row > j + 1
            new = rest - jnp.where(low, c0, 0.0) * (inv0 * r0) - jnp.where(low, c1, 0.0) * (inv1 * r1)
            rest = jnp.where(row == j + 1, jnp.broadcast_to(r1, shape), new)
        done.append(rest[:8])
        rest = rest[8:]
    mat = jnp.concatenate(done, axis=0)
    lanes = lax.broadcasted_iota(jnp.int32, (64, 128), 1)
    row = lax.broadcasted_iota(jnp.int32, (64, 128), 0)
    diag = jnp.sum(jnp.where(lanes == row, mat, 0.0), axis=1, keepdims=True)
    m_ref[...] = jnp.where((lanes >= 64) | (lanes >= row), mat * lax.rsqrt(diag), 0.0)


def kernel(
    plan, start_ref, blocks_ref, basis_ref, alpha_ref, beta_ref,
    q_ref, y_ref, r_ref, x_ref, m_ref, sums, held, buffers,
    ar_src, ar1, ar_s1, ar2, ar_s2, ar3, ar_s3, ar4, ar_send, ar_recv,
):
    r = lax.axis_index("row")
    c = lax.axis_index("col")
    z, k = r // 2, lax.rem(r, 2)
    cp, ch = lax.rem(c, 8), c // 8
    sibling = (z * 2 + (1 - k), c)
    mine, other = k * 16, (1 - k) * 16

    def along_z(o):
        there = lax.rem(z + o + NZ, NZ)
        return there, (there * 2 + k, c)

    def along_c(o):
        there = lax.rem(c + o, NC)
        return there, (r, there)

    barrier = pltpu.get_barrier_semaphore()
    for o in range(1, 16):
        pl.semaphore_signal(barrier, inc=1, device_id=along_z(o)[1], device_id_type=MESH)
        pl.semaphore_signal(barrier, inc=1, device_id=along_c(o)[1], device_id_type=MESH)
    pl.semaphore_signal(barrier, inc=1, device_id=sibling, device_id_type=MESH)

    def push(src, dst, send, recv, where):
        pltpu.make_async_remote_copy(
            src_ref=src, dst_ref=dst, send_sem=send, recv_sem=recv, device_id=where, device_id_type=MESH
        ).start()

    def settle(ref, sem):
        pltpu.make_async_copy(ref, ref, sem).wait()

    def reduce_1(s):
        ar_src[s] = x_ref[...].reshape(8, 8, 128)
        ar1[s, c] = ar_src[s, cp]
        for o in range(1, 16):
            there, where = along_c(o)
            push(ar_src.at[s, lax.rem(there, 8)], ar1.at[s, c], ar_send.at[s, 0], ar_recv.at[s, 0], where)

    def reduce_2(s):
        settle(ar1.at[s, pl.ds(0, 15)], ar_recv.at[s, 0])
        total = ar1[s, 0]
        for i in range(1, 16):
            total = total + ar1[s, i]
        ar_s1[s] = total
        push(ar_s1.at[s], ar2.at[s], ar_send.at[s, 1], ar_recv.at[s, 1], sibling)

    def reduce_3(s):
        settle(ar2.at[s], ar_recv.at[s, 1])
        ar_s2[s] = ar_s1[s] + ar2[s]
        ar3[s, z] = ar_s2[s]
        for o in FAR:
            push(ar_s2.at[s], ar3.at[s, z], ar_send.at[s, 2], ar_recv.at[s, 2], along_z(o)[1])

    def reduce_4(s):
        settle(ar3.at[s, pl.ds(0, 15)], ar_recv.at[s, 2])
        total = ar3[s, 0]
        for i in range(1, 16):
            total = total + ar3[s, i]
        ar_s3[s] = total
        ar4[s, cp] = total
        for o in range(1, 8):
            there = ch * 8 + lax.rem(cp + o, 8)
            push(ar_s3.at[s], ar4.at[s, cp], ar_send.at[s, 3], ar_recv.at[s, 3], (r, there))

    def reduce_5(s):
        settle(ar4.at[s, pl.ds(0, 7)], ar_recv.at[s, 3])
        x_ref[...] = ar4[s].reshape(64, 128) * (1.0 / (512 * 128))

    def reduce_end(s):
        settle(ar1.at[s, pl.ds(0, 15)], ar_send.at[s, 0])
        settle(ar2.at[s], ar_send.at[s, 1])
        settle(ar3.at[s, pl.ds(0, 15)], ar_send.at[s, 2])
        settle(ar4.at[s, pl.ds(0, 7)], ar_send.at[s, 3])

    def spread(t, value):
        u = buffers[t]
        value = value.astype(u["src"].dtype)
        u["src"][...] = value
        u["stripe"][c] = value
        u["colset"][mine] = value
        u["row_dst"][c] = jnp.zeros_like(value)
        for o, slot in ((6, 4), (-6, 3), (3, 2), (-3, 1)):
            sem = u["recv"].at[1 if slot > 2 else 0]
            push(u["src"], u["colset"].at[mine + slot], u["send"].at[0], sem, along_z(o)[1])
        push(u["src"], u["colset"].at[mine + 6], u["send"].at[0], u["recv"].at[2], along_z(1)[1])
        push(u["src"], u["colset"].at[mine + 11], u["send"].at[0], u["recv"].at[2], along_z(-1)[1])
        push(u["src"], u["colset"].at[mine + 5], u["send"].at[0], u["recv"].at[2], along_z(8)[1])
        for o in range(1, 16):
            push(u["src"], u["stripe"].at[c], u["send"].at[3], u["recv"].at[3], along_c(o)[1])

    def hop(t, first):
        u = buffers[t]
        settle(u["colset"].at[pl.ds(0, 2)], u["recv"].at[0 if first == 1 else 1])
        source = u["colset"].at[pl.ds(mine + first, 2)]
        for o, base in ((1, 6), (-1, 11)):
            target = u["colset"].at[pl.ds(mine + base + first, 2)]
            push(source, target, u["send"].at[0], u["recv"].at[2], along_z(o)[1])

    def relay(t, first, count):
        u = buffers[t]
        part = u["colset"].at[pl.ds(mine + first, count)]
        push(part, part, u["send"].at[4], u["recv"].at[4], sibling)

    def products(base, source, transposed):
        dims = (((1,), (1,)), ((), ())) if transposed else (((1,), (0,)), ((), ()))

        def one(p, total):
            value = source[plan[base + 64 + p]]
            matrix = blocks_ref[plan[base + p]]
            high = value.astype(BF16)
            part = lax.dot_general(high, matrix, dims, preferred_element_type=F32)
            if value.dtype == F32:
                low = (value - high.astype(F32)).astype(BF16)
                part = part + lax.dot_general(low, matrix, dims, preferred_element_type=F32)
            total = jnp.where(plan[base + 32 + p] > 0, total, 0.0) + part
            sums[p] = total
            return total

        lax.fori_loop(0, SLOTS, one, jnp.zeros((64, 128), F32), unroll=8)

    def backward(t):
        u = buffers[t]
        kind = u["src"].dtype
        settle(u["stripe"].at[pl.ds(0, 15)], u["recv"].at[3])
        products(128, u["stripe"], False)
        for i in range(NZ):
            u["pair_src"][i] = sums[plan[224 + other + i]].astype(kind)
        push(u["pair_src"], u["pair_dst"], u["send"].at[5], u["recv"].at[5], sibling)
        settle(u["pair_dst"], u["recv"].at[5])
        for i in range(15, 4, -1):
            u["zed_src"][i] = (sums[plan[224 + mine + i]] + u["pair_dst"][i].astype(F32)).astype(kind)
            if i == 11:
                push(u["zed_src"].at[pl.ds(11, 5)], u["near"].at[pl.ds(0, 5)], u["send"].at[6], u["recv"].at[6], along_z(1)[1])
            if i == 6:
                push(u["zed_src"].at[pl.ds(6, 5)], u["near"].at[pl.ds(5, 5)], u["send"].at[6], u["recv"].at[6], along_z(-1)[1])
        push(u["zed_src"].at[5], u["far"].at[4], u["send"].at[7], u["recv"].at[7], along_z(8)[1])
        for i in range(5):
            held[i] = sums[plan[224 + mine + i]] + u["pair_dst"][i].astype(F32)

    def forward(t):
        u = buffers[t]
        settle(u["colset"].at[pl.ds(0, 16)], u["recv"].at[4])
        products(0, u["colset"], True)
        for o in range(1, 16):
            there, where = along_c(o)
            u["row_src"][there] = sums[plan[96 + there]].astype(u["src"].dtype)
            push(u["row_src"].at[there], u["row_dst"].at[c], u["send"].at[8], u["recv"].at[8], where)

    def pass_on(t):
        u = buffers[t]
        settle(u["near"], u["recv"].at[6])
        for i, o in ((3, 6), (4, -6), (1, 3), (2, -3)):
            total = held[i] + u["near"][i].astype(F32) + u["near"][5 + i].astype(F32)
            u["zed_src"][i] = total.astype(u["src"].dtype)
            push(u["zed_src"].at[i], u["far"].at[i - 1], u["send"].at[7], u["recv"].at[7], along_z(o)[1])

    def collect(t):
        u = buffers[t]
        total = held[0] + u["near"][0].astype(F32) + u["near"][5].astype(F32) + sums[plan[96 + c]]
        settle(u["row_dst"].at[pl.ds(0, 15)], u["recv"].at[8])
        for i in range(NC):
            total = total + u["row_dst"][i].astype(F32)
        settle(u["far"], u["recv"].at[7])
        for i in range(5):
            total = total + u["far"][i].astype(F32)
        return total

    def operator_end(t):
        u = buffers[t]
        settle(u["colset"].at[pl.ds(0, 15)], u["send"].at[0])
        settle(u["stripe"].at[pl.ds(0, 15)], u["send"].at[3])
        settle(u["colset"].at[pl.ds(0, 16)], u["send"].at[4])
        settle(u["pair_dst"], u["send"].at[5])
        settle(u["near"], u["send"].at[6])
        settle(u["far"], u["send"].at[7])
        settle(u["row_dst"].at[pl.ds(0, 15)], u["send"].at[8])

    lanes = lax.broadcasted_iota(jnp.int32, (64, 64), 1)
    rows = lax.broadcasted_iota(jnp.int32, (64, 64), 0)
    eye = (lanes == rows).astype(F32)

    def factor_start():
        m_ref[:, 0:64] = x_ref[:, 0:64]
        m_ref[:, 64:128] = eye
        factor(m_ref)

    def factor_step(t):
        alpha_t = x_ref[:, 64:128]
        alpha_ref[t] = alpha_t
        m_ref[:, 0:64] = x_ref[:, 0:64] - nt(alpha_t, alpha_t)
        m_ref[:, 64:128] = eye
        factor(m_ref)
        beta_ref[t] = m_ref[:, 0:64]
        return alpha_t

    sums[SLOTS] = jnp.zeros((64, 128), F32)
    first = start_ref[...]
    x_ref[...] = nt(first, jnp.concatenate([first, first], axis=0))
    pl.semaphore_wait(barrier, 31)

    for s in range(ITERS):
        if s:
            x_ref[...] = nt(r_ref[...], jnp.concatenate([r_ref[...], q_ref[...]], axis=0))
        reduce_1(s)
        spread(s, r_ref[...] if s else first)
        hop(s, 1)
        reduce_2(s)
        hop(s, 3)
        relay(s, 0, 5)
        reduce_3(s)
        backward(s)
        settle(buffers[s]["colset"].at[pl.ds(0, 11)], buffers[s]["recv"].at[2])
        relay(s, 5, 11)
        forward(s)
        pass_on(s)
        reduce_4(s)
        reduce_5(s)
        if s == 0:
            factor_start()
            inverse = m_ref[:, 64:128]
            q_ref[...] = nn(inverse, first)
            y_ref[...] = nn(inverse, collect(s))
            r_ref[...] = y_ref[...]
        else:
            alpha_t = factor_step(s - 1)
            inverse = m_ref[:, 64:128]
            following = nn(inverse, r_ref[...] - nn(alpha_t, q_ref[...]))
            less = nn(alpha_t, y_ref[...])
            carried = nn(m_ref[:, 0:64], q_ref[...])
            y_ref[...] = nn(inverse, collect(s) - less)
            r_ref[...] = y_ref[...] - carried
            q_ref[...] = following
    x_ref[...] = nt(r_ref[...], jnp.concatenate([r_ref[...], q_ref[...]], axis=0))
    reduce_1(ITERS)
    for s in range(ITERS):
        operator_end(s)
        reduce_end(s)
    reduce_2(ITERS)
    reduce_3(ITERS)
    reduce_4(ITERS)
    reduce_5(ITERS)
    alpha_t = factor_step(ITERS - 1)
    basis_ref[...] = nn(m_ref[:, 64:128], r_ref[...] - nn(alpha_t, q_ref[...]))
    reduce_end(ITERS)


def shards(blocks, block_rows, block_cols, start):
    row_index = lax.axis_index("row")
    valid = block_rows < 512
    row_target = block_rows - row_index * NC
    col_owner = block_cols // NC
    away = lax.rem(col_owner // 2 - row_index // 2 + 3 * NZ, NZ)
    slot = jnp.sum(jnp.where(away[:, None] == jnp.array(REACH)[None, :], jnp.arange(NZ)[None, :], 0), axis=1)
    col_target = lax.rem(col_owner, 2) * NZ + slot
    plan = jnp.concatenate(
        plan_part(row_target, col_target, valid, NC) + plan_part(col_target, row_target, valid, 2 * NZ)
    )
    vmem = pl.BlockSpec(memory_space=pltpu.VMEM)
    tall = (ITERS + 1, 16, 8, 128)
    piece = (ITERS + 1, 8, 128)

    def buffer(kind):
        counts = dict(
            stripe=16, colset=32, pair_src=16, pair_dst=16, zed_src=16, near=10, far=5, row_src=16, row_dst=16
        )
        made = {name: pltpu.VMEM((count, 64, 128), kind) for name, count in counts.items()}
        made["src"] = pltpu.VMEM((64, 128), kind)
        made["send"] = pltpu.SemaphoreType.DMA((9,))
        made["recv"] = pltpu.SemaphoreType.DMA((9,))
        return made

    basis, alphas, betas = pl.pallas_call(
        kernel,
        out_shape=(
            jax.ShapeDtypeStruct((64, 128), F32),
            jax.ShapeDtypeStruct((ITERS, 64, 64), F32),
            jax.ShapeDtypeStruct((ITERS, 64, 64), F32),
        ),
        in_specs=[pl.BlockSpec(memory_space=pltpu.SMEM), vmem, vmem],
        out_specs=(vmem, vmem, vmem),
        scratch_shapes=[
            pltpu.VMEM((64, 128), F32),
            pltpu.VMEM((64, 128), F32),
            pltpu.VMEM((64, 128), F32),
            pltpu.VMEM((64, 128), F32),
            pltpu.VMEM((64, 128), F32),
            pltpu.VMEM((SLOTS + 1, 64, 128), F32),
            pltpu.VMEM((5, 64, 128), F32),
            [buffer(F32), buffer(BF16), buffer(BF16)],
            pltpu.VMEM((ITERS + 1, 8, 8, 128), F32),
            pltpu.VMEM(tall, F32),
            pltpu.VMEM(piece, F32),
            pltpu.VMEM(piece, F32),
            pltpu.VMEM(piece, F32),
            pltpu.VMEM(tall, F32),
            pltpu.VMEM(piece, F32),
            pltpu.VMEM((ITERS + 1, 8, 8, 128), F32),
            pltpu.SemaphoreType.DMA((ITERS + 1, 4)),
            pltpu.SemaphoreType.DMA((ITERS + 1, 4)),
        ],
        compiler_params=pltpu.CompilerParams(collective_id=0, has_side_effects=True, vmem_limit_bytes=36 << 20),
        name="lanczos",
    )(plan, start, blocks)
    return (basis, jnp.swapaxes(alphas, 1, 2), jnp.swapaxes(betas, 1, 2))


def solution(mesh):
    in_specs = (
        P(("row", "col"), None, None),
        P(("row", "col")),
        P(("row", "col")),
        P(None, ("row", "col")),
    )
    out_specs = (P(None, ("row", "col")), P(), P())
    return jax.shard_map(shards, mesh=mesh, in_specs=in_specs, out_specs=out_specs, check_vma=False)
```

```python
import jax
import jax.numpy as jnp
from jax import lax
from jax.experimental import pallas as pl
from jax.experimental.pallas import tpu as pltpu
from jax.sharding import PartitionSpec as P

ITERS = 3
HIGH = lax.Precision.HIGHEST
MESH = pl.DeviceIdType.MESH
F32 = jnp.float32
BF16 = jnp.bfloat16

NZ = 16
NC = 16
SLOTS = 32
HBM = pl.BlockSpec(memory_space=pltpu.HBM)
REACH = (0, 3, 13, 6, 10, 8, 15, 2, 12, 5, 9, 1, 4, 14, 7, 11)
FAR = (8, 7, 9, 6, 10, 5, 11, 4, 12, 3, 13, 2, 14, 1, 15)


def nt(a, b):
    return lax.dot_general(a, b, (((1,), (1,)), ((), ())), precision=HIGH, preferred_element_type=F32)


def nn(a, b):
    return lax.dot_general(a, b, (((1,), (0,)), ((), ())), precision=HIGH, preferred_element_type=F32)


def plan_part(target, source, valid, targets):
    across = lax.broadcasted_iota(jnp.int32, (SLOTS, SLOTS), 1).astype(F32)
    down = lax.broadcasted_iota(jnp.int32, (SLOTS, SLOTS), 0).astype(F32)
    diagonal = across == down

    def upright(row):
        return jnp.sum(jnp.where(diagonal, row, 0.0), axis=1, keepdims=True)

    target = jnp.where(valid, target, float(targets))
    key = target * SLOTS + across[:1]
    key_down, target_down = upright(key), upright(target)
    source_down = upright(jnp.where(valid, source, 0.0))
    rank = jnp.sum(jnp.where(key < key_down, 1.0, 0.0), axis=1, keepdims=True)

    def pick(column, place):
        return jnp.sum(jnp.where(place, column, 0.0), axis=0, keepdims=True)

    here = rank == across
    one = jnp.ones_like(rank)
    same = pick(target_down + 1.0, here) == pick(target_down + 1.0, rank + 1.0 == across)
    upto = pick(one, key_down < (across + 1.0) * SLOTS)
    some = pick(one, target_down == across)
    last = jnp.where(some > 0.0, upto - 1.0, float(SLOTS))
    rows = (pick(down[:, :1], here), jnp.where(same, 1.0, 0.0), pick(source_down, here), last)
    return [row.astype(jnp.int32) for row in rows]


def make_plan(rows_ref, cols_ref, plan_ref):
    r = lax.axis_index("row")
    z = r // 2
    row_index, col_index = rows_ref[...], cols_ref[...]
    valid = row_index < 512
    owner = lax.shift_right_logical(col_index, 4)
    away = (lax.shift_right_logical(owner, 1) - z + NZ) & 15
    slot = jnp.zeros_like(away)
    for i in range(1, NZ):
        slot = jnp.where(away == REACH[i], i, slot)
    row_target = jnp.clip(row_index - r * NC, 0, NC - 1).astype(F32)
    col_target = ((owner & 1) * NZ + slot).astype(F32)
    for base, part in (
        (0, plan_part(row_target, col_target, valid, SLOTS)),
        (4, plan_part(col_target, row_target, valid, SLOTS)),
    ):
        for i in range(4):
            plan_ref[base + i : base + i + 1, 0:SLOTS] = part[i]


def factor(m_ref):
    rest = m_ref[...]
    done = []
    for b in range(8):
        shape = rest.shape
        row = lax.broadcasted_iota(jnp.int32, shape, 0)
        cols = [jnp.broadcast_to(rest[:, 8 * b + i : 8 * b + i + 1], shape) for i in range(8)]
        for j in range(0, 8, 2):
            c0, c1 = cols[j], cols[j + 1]
            one, off, two = c0[j : j + 1], c0[j + 1 : j + 2], c1[j + 1 : j + 2]
            inv0 = 1.0 / one
            inv1 = one * (1.0 / (one * two - off * off))
            share = off * inv0
            r0 = rest[j : j + 1]
            r1 = rest[j + 1 : j + 2] - share * r0
            c1 = c1 - share * c0
            for i in range(j + 2, 8):
                cols[i] = cols[i] - c0 * (c0[i : i + 1] * inv0) - c1 * (c1[i : i + 1] * inv1)
            low = row > j + 1
            new = rest - jnp.where(low, c0, 0.0) * (inv0 * r0) - jnp.where(low, c1, 0.0) * (inv1 * r1)
            rest = jnp.where(row == j + 1, jnp.broadcast_to(r1, shape), new)
        done.append(rest[:8])
        rest = rest[8:]
    mat = jnp.concatenate(done, axis=0)
    lanes = lax.broadcasted_iota(jnp.int32, (64, 128), 1)
    row = lax.broadcasted_iota(jnp.int32, (64, 128), 0)
    diag = jnp.sum(jnp.where(lanes == row, mat, 0.0), axis=1, keepdims=True)
    m_ref[...] = jnp.where((lanes >= 64) | (lanes >= row), mat * lax.rsqrt(diag), 0.0)


def kernel(
    plan, start_hbm, blocks_hbm, basis_ref, alpha_ref, beta_ref,
    start_ref, blocks_ref, copy_sem, q_ref, y_ref, r_ref, x_ref, m_ref, sums, held, buffers,
    ar_src, ar1, ar_s1, ar2, ar_s2, ar3, ar_s3, ar4, ar_send, ar_recv,
):
    r = lax.axis_index("row")
    c = lax.axis_index("col")
    z, k = r // 2, lax.rem(r, 2)
    cp, ch = lax.rem(c, 8), c // 8
    sibling = (z * 2 + (1 - k), c)
    mine, other = k * 16, (1 - k) * 16

    def along_z(o):
        there = lax.rem(z + o + NZ, NZ)
        return there, (there * 2 + k, c)

    def along_c(o):
        there = lax.rem(c + o, NC)
        return there, (r, there)

    start_copy = pltpu.make_async_copy(start_hbm, start_ref, copy_sem.at[0])
    start_copy.start()
    blocks_copy = pltpu.make_async_copy(blocks_hbm, blocks_ref, copy_sem.at[1])
    blocks_copy.start()

    barrier = pltpu.get_barrier_semaphore()
    for o in range(1, 16):
        pl.semaphore_signal(barrier, inc=1, device_id=along_z(o)[1], device_id_type=MESH)
        pl.semaphore_signal(barrier, inc=1, device_id=along_c(o)[1], device_id_type=MESH)
    pl.semaphore_signal(barrier, inc=1, device_id=sibling, device_id_type=MESH)
    for o in range(1, 8):
        there = (sibling[0], ch * 8 + lax.rem(cp + o, 8))
        pl.semaphore_signal(barrier, inc=1, device_id=there, device_id_type=MESH)

    def push(src, dst, send, recv, where):
        pltpu.make_async_remote_copy(
            src_ref=src, dst_ref=dst, send_sem=send, recv_sem=recv, device_id=where, device_id_type=MESH
        ).start()

    def settle(ref, sem):
        pltpu.make_async_copy(ref, ref, sem).wait()

    def reduce_1(s):
        ar_src[s] = x_ref[...].reshape(8, 8, 128)
        ar1[s, c] = ar_src[s, cp]
        for o in range(1, 16):
            there, where = along_c(o)
            push(ar_src.at[s, lax.rem(there, 8)], ar1.at[s, c], ar_send.at[s, 0], ar_recv.at[s, 0], where)

    def reduce_2(s):
        settle(ar1.at[s, pl.ds(0, 15)], ar_recv.at[s, 0])
        total = ar1[s, 0]
        for i in range(1, 16):
            total = total + ar1[s, i]
        ar_s1[s, 0] = total[0:4]
        ar_s1[s, 1] = total[4:8]
        push(ar_s1.at[s, 1 - k], ar2.at[s], ar_send.at[s, 1], ar_recv.at[s, 1], sibling)

    def reduce_3(s):
        settle(ar2.at[s], ar_recv.at[s, 1])
        ar_s2[s] = ar_s1[s, k] + ar2[s]
        ar3[s, z] = ar_s2[s]
        for o in FAR:
            push(ar_s2.at[s], ar3.at[s, z], ar_send.at[s, 2], ar_recv.at[s, 2], along_z(o)[1])

    def reduce_4(s):
        settle(ar3.at[s, pl.ds(0, 15)], ar_recv.at[s, 2])
        total = ar3[s, 0]
        for i in range(1, 16):
            total = total + ar3[s, i]
        ar_s3[s] = total
        ar4[s, cp, k] = total
        for o in range(8):
            there = ch * 8 + lax.rem(cp + o, 8)
            for row in (r, sibling[0]) if o else (sibling[0],):
                push(ar_s3.at[s], ar4.at[s, cp, k], ar_send.at[s, 3], ar_recv.at[s, 3], (row, there))

    def reduce_5(s):
        settle(ar3.at[s, pl.ds(0, 15)], ar_recv.at[s, 3])
        for i in range(8):
            for h in range(2):
                x_ref[8 * i + 4 * h : 8 * i + 4 * h + 4] = ar4[s, i, h] * (1.0 / (512 * 128))

    def reduce_end(s):
        settle(ar1.at[s, pl.ds(0, 15)], ar_send.at[s, 0])
        settle(ar2.at[s], ar_send.at[s, 1])
        settle(ar3.at[s, pl.ds(0, 15)], ar_send.at[s, 2])
        settle(ar3.at[s, pl.ds(0, 15)], ar_send.at[s, 3])

    def spread(t, value):
        u = buffers[t]
        value = value.astype(u["src"].dtype)
        u["src"][...] = value
        u["stripe"][c] = value
        u["colset"][mine] = value
        u["row_dst"][c] = jnp.zeros_like(value)
        for o, slot in ((6, 4), (-6, 3), (3, 2), (-3, 1)):
            sem = u["recv"].at[1 if slot > 2 else 0]
            push(u["src"], u["colset"].at[mine + slot], u["send"].at[0], sem, along_z(o)[1])
        push(u["src"], u["colset"].at[mine + 6], u["send"].at[0], u["recv"].at[2], along_z(1)[1])
        push(u["src"], u["colset"].at[mine + 11], u["send"].at[0], u["recv"].at[2], along_z(-1)[1])
        push(u["src"], u["colset"].at[mine + 5], u["send"].at[0], u["recv"].at[2], along_z(8)[1])
        for o in range(1, 16):
            push(u["src"], u["stripe"].at[c], u["send"].at[3], u["recv"].at[3], along_c(o)[1])

    def hop(t, first):
        u = buffers[t]
        settle(u["colset"].at[pl.ds(0, 2)], u["recv"].at[0 if first == 1 else 1])
        source = u["colset"].at[pl.ds(mine + first, 2)]
        for o, base in ((1, 6), (-1, 11)):
            target = u["colset"].at[pl.ds(mine + base + first, 2)]
            push(source, target, u["send"].at[0], u["recv"].at[2], along_z(o)[1])

    def relay(t, first, count):
        u = buffers[t]
        part = u["colset"].at[pl.ds(mine + first, count)]
        push(part, part, u["send"].at[4], u["recv"].at[4], sibling)

    def products(base, source, transposed):
        dims = (((1,), (1,)), ((), ())) if transposed else (((1,), (0,)), ((), ()))

        def one(p, total):
            value = source[plan[base + 2, p]]
            matrix = blocks_ref[plan[base, p]]
            high = value.astype(BF16)
            part = lax.dot_general(high, matrix, dims, preferred_element_type=F32)
            if value.dtype == F32:
                low = (value - high.astype(F32)).astype(BF16)
                part = part + lax.dot_general(low, matrix, dims, preferred_element_type=F32)
            total = jnp.where(plan[base + 1, p] > 0, total, 0.0) + part
            sums[p] = total
            return total

        lax.fori_loop(0, SLOTS, one, jnp.zeros((64, 128), F32), unroll=8)

    def backward(t):
        u = buffers[t]
        kind = u["src"].dtype
        settle(u["stripe"].at[pl.ds(0, 15)], u["recv"].at[3])
        products(4, u["stripe"], False)
        for i in range(NZ):
            u["pair_src"][i] = sums[plan[7, other + i]].astype(kind)
        push(u["pair_src"], u["pair_dst"], u["send"].at[5], u["recv"].at[5], sibling)
        settle(u["pair_dst"], u["recv"].at[5])
        for i in range(15, 4, -1):
            u["zed_src"][i] = (sums[plan[7, mine + i]] + u["pair_dst"][i].astype(F32)).astype(kind)
            if i == 11:
                push(u["zed_src"].at[pl.ds(11, 5)], u["near"].at[pl.ds(0, 5)], u["send"].at[6], u["recv"].at[6], along_z(1)[1])
            if i == 6:
                push(u["zed_src"].at[pl.ds(6, 5)], u["near"].at[pl.ds(5, 5)], u["send"].at[6], u["recv"].at[6], along_z(-1)[1])
        push(u["zed_src"].at[5], u["far"].at[4], u["send"].at[7], u["recv"].at[7], along_z(8)[1])
        for i in range(5):
            held[i] = sums[plan[7, mine + i]] + u["pair_dst"][i].astype(F32)

    def forward(t):
        u = buffers[t]
        settle(u["colset"].at[pl.ds(0, 16)], u["recv"].at[4])
        products(0, u["colset"], True)
        for o in range(1, 16):
            there, where = along_c(o)
            u["row_src"][there] = sums[plan[3, there]].astype(u["src"].dtype)
            push(u["row_src"].at[there], u["row_dst"].at[c], u["send"].at[8], u["recv"].at[8], where)

    def pass_on(t):
        u = buffers[t]
        settle(u["near"], u["recv"].at[6])
        for i, o in ((3, 6), (4, -6), (1, 3), (2, -3)):
            total = held[i] + u["near"][i].astype(F32) + u["near"][5 + i].astype(F32)
            u["zed_src"][i] = total.astype(u["src"].dtype)
            push(u["zed_src"].at[i], u["far"].at[i - 1], u["send"].at[7], u["recv"].at[7], along_z(o)[1])

    def collect(t):
        u = buffers[t]
        total = held[0] + u["near"][0].astype(F32) + u["near"][5].astype(F32) + sums[plan[3, c]]
        settle(u["row_dst"].at[pl.ds(0, 15)], u["recv"].at[8])
        for i in range(NC):
            total = total + u["row_dst"][i].astype(F32)
        settle(u["far"], u["recv"].at[7])
        for i in range(5):
            total = total + u["far"][i].astype(F32)
        return total

    def operator_end(t):
        u = buffers[t]
        settle(u["colset"].at[pl.ds(0, 15)], u["send"].at[0])
        settle(u["stripe"].at[pl.ds(0, 15)], u["send"].at[3])
        settle(u["colset"].at[pl.ds(0, 16)], u["send"].at[4])
        settle(u["pair_dst"], u["send"].at[5])
        settle(u["near"], u["send"].at[6])
        settle(u["far"], u["send"].at[7])
        settle(u["row_dst"].at[pl.ds(0, 15)], u["send"].at[8])

    lanes = lax.broadcasted_iota(jnp.int32, (64, 64), 1)
    rows = lax.broadcasted_iota(jnp.int32, (64, 64), 0)
    eye = (lanes == rows).astype(F32)

    def factor_start():
        m_ref[:, 0:64] = x_ref[:, 0:64]
        m_ref[:, 64:128] = eye
        factor(m_ref)

    def factor_step(t):
        alpha_t = x_ref[:, 64:128]
        alpha_ref[t] = alpha_t
        m_ref[:, 0:64] = x_ref[:, 0:64] - nt(alpha_t, alpha_t)
        m_ref[:, 64:128] = eye
        factor(m_ref)
        beta_ref[t] = m_ref[:, 0:64]
        return alpha_t

    sums[SLOTS] = jnp.zeros((64, 128), F32)
    start_copy.wait()
    first = start_ref[...]
    x_ref[...] = nt(first, jnp.concatenate([first, first], axis=0))
    blocks_copy.wait()
    pl.semaphore_wait(barrier, 38)

    for s in range(ITERS):
        if s:
            x_ref[...] = nt(r_ref[...], jnp.concatenate([r_ref[...], q_ref[...]], axis=0))
        reduce_1(s)
        spread(s, r_ref[...] if s else first)
        hop(s, 1)
        reduce_2(s)
        hop(s, 3)
        relay(s, 0, 5)
        reduce_3(s)
        backward(s)
        settle(buffers[s]["colset"].at[pl.ds(0, 11)], buffers[s]["recv"].at[2])
        relay(s, 5, 11)
        forward(s)
        pass_on(s)
        reduce_4(s)
        reduce_5(s)
        if s == 0:
            factor_start()
            inverse = m_ref[:, 64:128]
            q_ref[...] = nn(inverse, first)
            y_ref[...] = nn(inverse, collect(s))
            r_ref[...] = y_ref[...]
        else:
            alpha_t = factor_step(s - 1)
            inverse = m_ref[:, 64:128]
            following = nn(inverse, r_ref[...] - nn(alpha_t, q_ref[...]))
            less = nn(alpha_t, y_ref[...])
            carried = nn(m_ref[:, 0:64], q_ref[...])
            y_ref[...] = nn(inverse, collect(s) - less)
            r_ref[...] = y_ref[...] - carried
            q_ref[...] = following
    x_ref[...] = nt(r_ref[...], jnp.concatenate([r_ref[...], q_ref[...]], axis=0))
    reduce_1(ITERS)
    for s in range(ITERS):
        operator_end(s)
        reduce_end(s)
    reduce_2(ITERS)
    reduce_3(ITERS)
    reduce_4(ITERS)
    reduce_5(ITERS)
    alpha_t = factor_step(ITERS - 1)
    basis_ref[...] = nn(m_ref[:, 64:128], r_ref[...] - nn(alpha_t, q_ref[...]))
    reduce_end(ITERS)


def finish(basis_ref, alpha_ref, beta_ref, basis_out, alpha_out, beta_out):
    basis_out[...] = basis_ref[...]
    for t in range(ITERS):
        alpha_out[t] = alpha_ref[t].T
        beta_out[t] = beta_ref[t].T


def shards(blocks, block_rows, block_cols, start):
    vmem = pl.BlockSpec(memory_space=pltpu.VMEM)
    shapes = (
        jax.ShapeDtypeStruct((64, 128), F32),
        jax.ShapeDtypeStruct((ITERS, 64, 64), F32),
        jax.ShapeDtypeStruct((ITERS, 64, 64), F32),
    )
    half = (ITERS + 1, 4, 128)

    def buffer(kind):
        counts = dict(
            stripe=16, colset=32, pair_src=16, pair_dst=16, zed_src=16, near=10, far=5, row_src=16, row_dst=16
        )
        made = {name: pltpu.VMEM((count, 64, 128), kind) for name, count in counts.items()}
        made["src"] = pltpu.VMEM((64, 128), kind)
        made["send"] = pltpu.SemaphoreType.DMA((9,))
        made["recv"] = pltpu.SemaphoreType.DMA((9,))
        return made

    plan = pl.pallas_call(
        make_plan,
        out_shape=jax.ShapeDtypeStruct((8, 128), jnp.int32),
        in_specs=[vmem, vmem],
        out_specs=vmem,
        compiler_params=pltpu.CompilerParams(vmem_limit_bytes=60 << 20),
        name="plan",
    )(block_rows.reshape(1, SLOTS), block_cols.reshape(1, SLOTS))
    basis, alphas, betas = pl.pallas_call(
        kernel,
        out_shape=shapes,
        in_specs=[pl.BlockSpec(memory_space=pltpu.SMEM), HBM, HBM],
        out_specs=(vmem, vmem, vmem),
        scratch_shapes=[
            pltpu.VMEM((64, 128), F32),
            pltpu.VMEM((SLOTS, 128, 128), BF16),
            pltpu.SemaphoreType.DMA((2,)),
            pltpu.VMEM((64, 128), F32),
            pltpu.VMEM((64, 128), F32),
            pltpu.VMEM((64, 128), F32),
            pltpu.VMEM((64, 128), F32),
            pltpu.VMEM((64, 128), F32),
            pltpu.VMEM((SLOTS + 1, 64, 128), F32),
            pltpu.VMEM((5, 64, 128), F32),
            [buffer(F32), buffer(BF16), buffer(BF16)],
            pltpu.VMEM((ITERS + 1, 8, 8, 128), F32),
            pltpu.VMEM((ITERS + 1, 16, 8, 128), F32),
            pltpu.VMEM((ITERS + 1, 2, 4, 128), F32),
            pltpu.VMEM(half, F32),
            pltpu.VMEM(half, F32),
            pltpu.VMEM((ITERS + 1, 16, 4, 128), F32),
            pltpu.VMEM(half, F32),
            pltpu.VMEM((ITERS + 1, 8, 2, 4, 128), F32),
            pltpu.SemaphoreType.DMA((ITERS + 1, 4)),
            pltpu.SemaphoreType.DMA((ITERS + 1, 4)),
        ],
        compiler_params=pltpu.CompilerParams(collective_id=0, has_side_effects=True, vmem_limit_bytes=60 << 20),
        name="lanczos",
    )(plan, start, blocks)
    return pl.pallas_call(
        finish,
        out_shape=shapes,
        in_specs=[vmem] * 3,
        out_specs=(vmem,) * 3,
        name="finish",
    )(basis, alphas, betas)


def solution(mesh):
    in_specs = (
        P(("row", "col"), None, None),
        P(("row", "col")),
        P(("row", "col")),
        P(None, ("row", "col")),
    )
    out_specs = (P(None, ("row", "col")), P(), P())
    return jax.shard_map(shards, mesh=mesh, in_specs=in_specs, out_specs=out_specs, check_vma=False)
```

```python
import jax
import jax.numpy as jnp
from jax import lax
from jax.experimental import pallas as pl
from jax.experimental.pallas import tpu as pltpu
from jax.sharding import PartitionSpec as P

ITERS = 3
HIGH = lax.Precision.HIGHEST
MESH = pl.DeviceIdType.MESH
F32 = jnp.float32
BF16 = jnp.bfloat16

NZ = 16
NC = 16
SLOTS = 32
HBM = pl.BlockSpec(memory_space=pltpu.HBM)
REACH = (0, 3, 13, 6, 10, 8, 15, 2, 12, 5, 9, 1, 4, 14, 7, 11)
FAR = (8, 7, 9, 6, 10, 5, 11, 4, 12, 3, 13, 2, 14, 1, 15)


def nt(a, b):
    return lax.dot_general(a, b, (((1,), (1,)), ((), ())), precision=HIGH, preferred_element_type=F32)


def nn(a, b):
    return lax.dot_general(a, b, (((1,), (0,)), ((), ())), precision=HIGH, preferred_element_type=F32)


def plan_part(target, source, valid, targets):
    across = lax.broadcasted_iota(jnp.int32, (SLOTS, SLOTS), 1)
    down = lax.broadcasted_iota(jnp.int32, (SLOTS, SLOTS), 0)
    diagonal = across == down

    def upright(row):
        return jnp.sum(jnp.where(diagonal, row, 0), axis=1, keepdims=True)

    def pick(column, place):
        return jnp.sum(jnp.where(place, column, 0), axis=0, keepdims=True)

    target = jnp.where(valid, target, targets)
    key = target * SLOTS + across[:1]
    key_down, target_down = upright(key), upright(target)
    source_down = upright(jnp.where(valid, source, 0))
    rank = jnp.sum(jnp.where(key < key_down, 1, 0), axis=1, keepdims=True)
    here = rank == across
    one = jnp.ones_like(rank)
    same = pick(target_down + 1, here) == pick(target_down + 1, rank + 1 == across)
    upto = pick(one, key_down < (across + 1) * SLOTS)
    some = pick(one, target_down == across)
    last = jnp.where(some > 0, upto - 1, SLOTS)
    return (pick(down[:, :1], here), jnp.where(same, 1, 0), pick(source_down, here), last)


def factor(m_ref):
    rest = m_ref[...]
    done = []
    for b in range(8):
        shape = rest.shape
        row = lax.broadcasted_iota(jnp.int32, shape, 0)
        cols = [jnp.broadcast_to(rest[:, 8 * b + i : 8 * b + i + 1], shape) for i in range(8)]
        for j in range(0, 8, 2):
            c0, c1 = cols[j], cols[j + 1]
            one, off, two = c0[j : j + 1], c0[j + 1 : j + 2], c1[j + 1 : j + 2]
            inv0 = 1.0 / one
            inv1 = one * (1.0 / (one * two - off * off))
            share = off * inv0
            r0 = rest[j : j + 1]
            r1 = rest[j + 1 : j + 2] - share * r0
            c1 = c1 - share * c0
            for i in range(j + 2, 8):
                cols[i] = cols[i] - c0 * (c0[i : i + 1] * inv0) - c1 * (c1[i : i + 1] * inv1)
            low = row > j + 1
            new = rest - jnp.where(low, c0, 0.0) * (inv0 * r0) - jnp.where(low, c1, 0.0) * (inv1 * r1)
            rest = jnp.where(row == j + 1, jnp.broadcast_to(r1, shape), new)
        done.append(rest[:8])
        rest = rest[8:]
    mat = jnp.concatenate(done, axis=0)
    lanes = lax.broadcasted_iota(jnp.int32, (64, 128), 1)
    row = lax.broadcasted_iota(jnp.int32, (64, 128), 0)
    diag = jnp.sum(jnp.where(lanes == row, mat, 0.0), axis=1, keepdims=True)
    m_ref[...] = jnp.where((lanes >= 64) | (lanes >= row), mat * lax.rsqrt(diag), 0.0)


def kernel(
    rows_ref, cols_ref, start_hbm, blocks_hbm, basis_ref, alpha_ref, beta_ref,
    start_ref, blocks_ref, plan_ref, table, copy_sem, q_ref, y_ref, r_ref, x_ref, m_ref, sums, held, buffers,
    ar_src, ar1, ar_s1, ar2, ar_s2, ar3, ar_s3, ar4, ar_send, ar_recv,
):
    r = lax.axis_index("row")
    c = lax.axis_index("col")
    z, k = r // 2, lax.rem(r, 2)
    cp, ch = lax.rem(c, 8), c // 8
    sibling = (z * 2 + (1 - k), c)
    mine, other = k * 16, (1 - k) * 16

    def along_z(o):
        there = lax.rem(z + o + NZ, NZ)
        return there, (there * 2 + k, c)

    def along_c(o):
        there = lax.rem(c + o, NC)
        return there, (r, there)

    start_copy = pltpu.make_async_copy(start_hbm, start_ref, copy_sem.at[0])
    start_copy.start()
    blocks_copy = pltpu.make_async_copy(blocks_hbm, blocks_ref, copy_sem.at[1])
    blocks_copy.start()

    barrier = pltpu.get_barrier_semaphore()
    for o in range(1, 16):
        pl.semaphore_signal(barrier, inc=1, device_id=along_z(o)[1], device_id_type=MESH)
        pl.semaphore_signal(barrier, inc=1, device_id=along_c(o)[1], device_id_type=MESH)
    pl.semaphore_signal(barrier, inc=1, device_id=sibling, device_id_type=MESH)
    for o in range(1, 8):
        there = (sibling[0], ch * 8 + lax.rem(cp + o, 8))
        pl.semaphore_signal(barrier, inc=1, device_id=there, device_id_type=MESH)

    def plan(row, i):
        return jnp.clip(table[row, i], 0, {3: SLOTS, 6: NC - 1, 7: SLOTS}.get(row, SLOTS - 1))

    def push(src, dst, send, recv, where):
        pltpu.make_async_remote_copy(
            src_ref=src, dst_ref=dst, send_sem=send, recv_sem=recv, device_id=where, device_id_type=MESH
        ).start()

    def settle(ref, sem):
        pltpu.make_async_copy(ref, ref, sem).wait()

    def reduce_1(s):
        ar_src[s] = x_ref[...].reshape(8, 8, 128)
        ar1[s, c] = ar_src[s, cp]
        for o in range(1, 16):
            there, where = along_c(o)
            push(ar_src.at[s, lax.rem(there, 8)], ar1.at[s, c], ar_send.at[s, 0], ar_recv.at[s, 0], where)

    def reduce_2(s):
        settle(ar1.at[s, pl.ds(0, 15)], ar_recv.at[s, 0])
        total = ar1[s, 0]
        for i in range(1, 16):
            total = total + ar1[s, i]
        ar_s1[s, 0] = total[0:4]
        ar_s1[s, 1] = total[4:8]
        push(ar_s1.at[s, 1 - k], ar2.at[s], ar_send.at[s, 1], ar_recv.at[s, 1], sibling)

    def reduce_3(s):
        settle(ar2.at[s], ar_recv.at[s, 1])
        ar_s2[s] = ar_s1[s, k] + ar2[s]
        ar3[s, z] = ar_s2[s]
        for o in FAR:
            push(ar_s2.at[s], ar3.at[s, z], ar_send.at[s, 2], ar_recv.at[s, 2], along_z(o)[1])

    def reduce_4(s):
        settle(ar3.at[s, pl.ds(0, 15)], ar_recv.at[s, 2])
        total = ar3[s, 0]
        for i in range(1, 16):
            total = total + ar3[s, i]
        ar_s3[s] = total
        ar4[s, cp, k] = total
        for o in range(8):
            there = ch * 8 + lax.rem(cp + o, 8)
            for row in (r, sibling[0]) if o else (sibling[0],):
                push(ar_s3.at[s], ar4.at[s, cp, k], ar_send.at[s, 3], ar_recv.at[s, 3], (row, there))

    def reduce_5(s):
        settle(ar3.at[s, pl.ds(0, 15)], ar_recv.at[s, 3])
        for i in range(8):
            for h in range(2):
                x_ref[8 * i + 4 * h : 8 * i + 4 * h + 4] = ar4[s, i, h] * (1.0 / (512 * 128))

    def reduce_end(s):
        settle(ar1.at[s, pl.ds(0, 15)], ar_send.at[s, 0])
        settle(ar2.at[s], ar_send.at[s, 1])
        settle(ar3.at[s, pl.ds(0, 15)], ar_send.at[s, 2])
        settle(ar3.at[s, pl.ds(0, 15)], ar_send.at[s, 3])

    def spread(t, value):
        u = buffers[t]
        value = value.astype(u["src"].dtype)
        u["src"][...] = value
        u["stripe"][c] = value
        u["colset"][mine] = value
        u["row_dst"][c] = jnp.zeros_like(value)
        for o, slot in ((6, 4), (-6, 3), (3, 2), (-3, 1)):
            sem = u["recv"].at[1 if slot > 2 else 0]
            push(u["src"], u["colset"].at[mine + slot], u["send"].at[0], sem, along_z(o)[1])
        push(u["src"], u["colset"].at[mine + 6], u["send"].at[0], u["recv"].at[2], along_z(1)[1])
        push(u["src"], u["colset"].at[mine + 11], u["send"].at[0], u["recv"].at[2], along_z(-1)[1])
        push(u["src"], u["colset"].at[mine + 5], u["send"].at[0], u["recv"].at[2], along_z(8)[1])
        for o in range(1, 16):
            push(u["src"], u["stripe"].at[c], u["send"].at[3], u["recv"].at[3], along_c(o)[1])

    def hop(t, first):
        u = buffers[t]
        settle(u["colset"].at[pl.ds(0, 2)], u["recv"].at[0 if first == 1 else 1])
        source = u["colset"].at[pl.ds(mine + first, 2)]
        for o, base in ((1, 6), (-1, 11)):
            target = u["colset"].at[pl.ds(mine + base + first, 2)]
            push(source, target, u["send"].at[0], u["recv"].at[2], along_z(o)[1])

    def relay(t, first, count):
        u = buffers[t]
        part = u["colset"].at[pl.ds(mine + first, count)]
        push(part, part, u["send"].at[4], u["recv"].at[4], sibling)

    def products(base, source, transposed):
        dims = (((1,), (1,)), ((), ())) if transposed else (((1,), (0,)), ((), ()))

        def one(p, total):
            value = source[plan(base + 2, p)]
            matrix = blocks_ref[plan(base, p)]
            high = value.astype(BF16)
            part = lax.dot_general(high, matrix, dims, preferred_element_type=F32)
            if value.dtype == F32:
                low = (value - high.astype(F32)).astype(BF16)
                part = part + lax.dot_general(low, matrix, dims, preferred_element_type=F32)
            total = jnp.where(plan(base + 1, p) > 0, total, 0.0) + part
            sums[p] = total
            return total

        lax.fori_loop(0, SLOTS, one, jnp.zeros((64, 128), F32), unroll=8)

    def backward(t):
        u = buffers[t]
        kind = u["src"].dtype
        settle(u["stripe"].at[pl.ds(0, 15)], u["recv"].at[3])
        products(4, u["stripe"], False)
        for i in range(NZ):
            u["pair_src"][i] = sums[plan(7, other + i)].astype(kind)
        push(u["pair_src"], u["pair_dst"], u["send"].at[5], u["recv"].at[5], sibling)
        settle(u["pair_dst"], u["recv"].at[5])
        for i in range(15, 4, -1):
            u["zed_src"][i] = (sums[plan(7, mine + i)] + u["pair_dst"][i].astype(F32)).astype(kind)
            if i == 11:
                push(u["zed_src"].at[pl.ds(11, 5)], u["near"].at[pl.ds(0, 5)], u["send"].at[6], u["recv"].at[6], along_z(1)[1])
            if i == 6:
                push(u["zed_src"].at[pl.ds(6, 5)], u["near"].at[pl.ds(5, 5)], u["send"].at[6], u["recv"].at[6], along_z(-1)[1])
        push(u["zed_src"].at[5], u["far"].at[4], u["send"].at[7], u["recv"].at[7], along_z(8)[1])
        for i in range(5):
            held[i] = sums[plan(7, mine + i)] + u["pair_dst"][i].astype(F32)

    def forward(t):
        u = buffers[t]
        settle(u["colset"].at[pl.ds(0, 16)], u["recv"].at[4])
        products(0, u["colset"], True)
        for o in range(1, 16):
            there, where = along_c(o)
            u["row_src"][there] = sums[plan(3, there)].astype(u["src"].dtype)
            push(u["row_src"].at[there], u["row_dst"].at[c], u["send"].at[8], u["recv"].at[8], where)

    def pass_on(t):
        u = buffers[t]
        settle(u["near"], u["recv"].at[6])
        for i, o in ((3, 6), (4, -6), (1, 3), (2, -3)):
            total = held[i] + u["near"][i].astype(F32) + u["near"][5 + i].astype(F32)
            u["zed_src"][i] = total.astype(u["src"].dtype)
            push(u["zed_src"].at[i], u["far"].at[i - 1], u["send"].at[7], u["recv"].at[7], along_z(o)[1])

    def collect(t):
        u = buffers[t]
        total = held[0] + u["near"][0].astype(F32) + u["near"][5].astype(F32) + sums[plan(3, c)]
        settle(u["row_dst"].at[pl.ds(0, 15)], u["recv"].at[8])
        for i in range(NC):
            total = total + u["row_dst"][i].astype(F32)
        settle(u["far"], u["recv"].at[7])
        for i in range(5):
            total = total + u["far"][i].astype(F32)
        return total

    def operator_end(t):
        u = buffers[t]
        settle(u["colset"].at[pl.ds(0, 15)], u["send"].at[0])
        settle(u["stripe"].at[pl.ds(0, 15)], u["send"].at[3])
        settle(u["colset"].at[pl.ds(0, 16)], u["send"].at[4])
        settle(u["pair_dst"], u["send"].at[5])
        settle(u["near"], u["send"].at[6])
        settle(u["far"], u["send"].at[7])
        settle(u["row_dst"].at[pl.ds(0, 15)], u["send"].at[8])

    lanes = lax.broadcasted_iota(jnp.int32, (64, 64), 1)
    rows = lax.broadcasted_iota(jnp.int32, (64, 64), 0)
    eye = (lanes == rows).astype(F32)

    def factor_start():
        m_ref[:, 0:64] = x_ref[:, 0:64]
        m_ref[:, 64:128] = eye
        factor(m_ref)

    def factor_step(t):
        alpha_t = x_ref[:, 64:128]
        alpha_ref[t] = alpha_t
        m_ref[:, 0:64] = x_ref[:, 0:64] - nt(alpha_t, alpha_t)
        m_ref[:, 64:128] = eye
        factor(m_ref)
        beta_ref[t] = m_ref[:, 0:64]
        return alpha_t

    sums[SLOTS] = jnp.zeros((64, 128), F32)
    plan_ref[...] = jnp.zeros((8, 128), jnp.int32)
    row_index, col_index = rows_ref[...], cols_ref[...]
    valid = row_index < 512
    owner = lax.shift_right_logical(col_index, 4)
    away = (lax.shift_right_logical(owner, 1) - z + NZ) & 15
    slot = jnp.zeros_like(away)
    for i in range(1, NZ):
        slot = jnp.where(away == REACH[i], i, slot)
    row_target = jnp.clip(row_index - r * NC, 0, NC - 1)
    col_target = (owner & 1) * NZ + slot
    for base, part in (
        (0, plan_part(row_target, col_target, valid, SLOTS)),
        (4, plan_part(col_target, row_target, valid, SLOTS)),
    ):
        for i in range(4):
            plan_ref[base + i : base + i + 1, 0:SLOTS] = part[i]
    plan_copy = pltpu.make_async_copy(plan_ref, table, copy_sem.at[2])
    plan_copy.start()
    start_copy.wait()
    first = start_ref[...]
    x_ref[...] = nt(first, jnp.concatenate([first, first], axis=0))
    blocks_copy.wait()
    plan_copy.wait()
    pl.semaphore_wait(barrier, 38)

    for s in range(ITERS):
        if s:
            x_ref[...] = nt(r_ref[...], jnp.concatenate([r_ref[...], q_ref[...]], axis=0))
        reduce_1(s)
        spread(s, r_ref[...] if s else first)
        hop(s, 1)
        reduce_2(s)
        hop(s, 3)
        relay(s, 0, 5)
        reduce_3(s)
        backward(s)
        settle(buffers[s]["colset"].at[pl.ds(0, 11)], buffers[s]["recv"].at[2])
        relay(s, 5, 11)
        forward(s)
        pass_on(s)
        reduce_4(s)
        reduce_5(s)
        if s == 0:
            factor_start()
            inverse = m_ref[:, 64:128]
            q_ref[...] = nn(inverse, first)
            y_ref[...] = nn(inverse, collect(s))
            r_ref[...] = y_ref[...]
        else:
            alpha_t = factor_step(s - 1)
            inverse = m_ref[:, 64:128]
            following = nn(inverse, r_ref[...] - nn(alpha_t, q_ref[...]))
            less = nn(alpha_t, y_ref[...])
            carried = nn(m_ref[:, 0:64], q_ref[...])
            y_ref[...] = nn(inverse, collect(s) - less)
            r_ref[...] = y_ref[...] - carried
            q_ref[...] = following
    x_ref[...] = nt(r_ref[...], jnp.concatenate([r_ref[...], q_ref[...]], axis=0))
    reduce_1(ITERS)
    for s in range(ITERS):
        operator_end(s)
        reduce_end(s)
    reduce_2(ITERS)
    reduce_3(ITERS)
    reduce_4(ITERS)
    reduce_5(ITERS)
    alpha_t = factor_step(ITERS - 1)
    basis_ref[...] = nn(m_ref[:, 64:128], r_ref[...] - nn(alpha_t, q_ref[...]))
    reduce_end(ITERS)


def finish(basis_ref, alpha_ref, beta_ref, basis_out, alpha_out, beta_out):
    basis_out[...] = basis_ref[...]
    for t in range(ITERS):
        alpha_out[t] = alpha_ref[t].T
        beta_out[t] = beta_ref[t].T


def shards(blocks, block_rows, block_cols, start):
    vmem = pl.BlockSpec(memory_space=pltpu.VMEM)
    shapes = (
        jax.ShapeDtypeStruct((64, 128), F32),
        jax.ShapeDtypeStruct((ITERS, 64, 64), F32),
        jax.ShapeDtypeStruct((ITERS, 64, 64), F32),
    )
    half = (ITERS + 1, 4, 128)

    def buffer(kind):
        counts = dict(
            stripe=16, colset=32, pair_src=16, pair_dst=16, zed_src=16, near=10, far=5, row_src=16, row_dst=16
        )
        made = {name: pltpu.VMEM((count, 64, 128), kind) for name, count in counts.items()}
        made["src"] = pltpu.VMEM((64, 128), kind)
        made["send"] = pltpu.SemaphoreType.DMA((9,))
        made["recv"] = pltpu.SemaphoreType.DMA((9,))
        return made

    basis, alphas, betas = pl.pallas_call(
        kernel,
        out_shape=shapes,
        in_specs=[vmem, vmem, HBM, HBM],
        out_specs=(vmem, vmem, vmem),
        scratch_shapes=[
            pltpu.VMEM((64, 128), F32),
            pltpu.VMEM((SLOTS, 128, 128), BF16),
            pltpu.VMEM((8, 128), jnp.int32),
            pltpu.SMEM((8, 128), jnp.int32),
            pltpu.SemaphoreType.DMA((3,)),
            pltpu.VMEM((64, 128), F32),
            pltpu.VMEM((64, 128), F32),
            pltpu.VMEM((64, 128), F32),
            pltpu.VMEM((64, 128), F32),
            pltpu.VMEM((64, 128), F32),
            pltpu.VMEM((SLOTS + 1, 64, 128), F32),
            pltpu.VMEM((5, 64, 128), F32),
            [buffer(F32), buffer(BF16), buffer(BF16)],
            pltpu.VMEM((ITERS + 1, 8, 8, 128), F32),
            pltpu.VMEM((ITERS + 1, 16, 8, 128), F32),
            pltpu.VMEM((ITERS + 1, 2, 4, 128), F32),
            pltpu.VMEM(half, F32),
            pltpu.VMEM(half, F32),
            pltpu.VMEM((ITERS + 1, 16, 4, 128), F32),
            pltpu.VMEM(half, F32),
            pltpu.VMEM((ITERS + 1, 8, 2, 4, 128), F32),
            pltpu.SemaphoreType.DMA((ITERS + 1, 4)),
            pltpu.SemaphoreType.DMA((ITERS + 1, 4)),
        ],
        compiler_params=pltpu.CompilerParams(collective_id=0, has_side_effects=True, vmem_limit_bytes=60 << 20),
        name="lanczos",
    )(block_rows.reshape(1, SLOTS), block_cols.reshape(1, SLOTS), start, blocks)
    return pl.pallas_call(
        finish,
        out_shape=shapes,
        in_specs=[vmem] * 3,
        out_specs=(vmem,) * 3,
        name="finish",
    )(basis, alphas, betas)


def solution(mesh):
    in_specs = (
        P(("row", "col"), None, None),
        P(("row", "col")),
        P(("row", "col")),
        P(None, ("row", "col")),
    )
    out_specs = (P(None, ("row", "col")), P(), P())
    return jax.shard_map(shards, mesh=mesh, in_specs=in_specs, out_specs=out_specs, check_vma=False)
```

```python
import jax
import jax.numpy as jnp
from jax import lax
from jax.experimental import pallas as pl
from jax.experimental.pallas import tpu as pltpu
from jax.sharding import PartitionSpec as P

ITERS = 3
HIGH = lax.Precision.HIGHEST
MESH = pl.DeviceIdType.MESH
F32 = jnp.float32
BF16 = jnp.bfloat16

NZ = 16
NC = 16
SLOTS = 32
HBM = pl.BlockSpec(memory_space=pltpu.HBM)
REACH = (0, 3, 13, 6, 10, 8, 15, 2, 12, 5, 9, 1, 4, 14, 7, 11)
FAR = (8, 7, 9, 6, 10, 5, 11, 4, 12, 3, 13, 2, 14, 1, 15)


def nt(a, b):
    return lax.dot_general(a, b, (((1,), (1,)), ((), ())), precision=HIGH, preferred_element_type=F32)


def nn(a, b):
    return lax.dot_general(a, b, (((1,), (0,)), ((), ())), precision=HIGH, preferred_element_type=F32)


def plan_part(target, source, valid, targets):
    across = lax.broadcasted_iota(jnp.int32, (SLOTS, SLOTS), 1)
    down = lax.broadcasted_iota(jnp.int32, (SLOTS, SLOTS), 0)
    diagonal = across == down

    def upright(row):
        return jnp.sum(jnp.where(diagonal, row, 0), axis=1, keepdims=True)

    def pick(column, place):
        return jnp.sum(jnp.where(place, column, 0), axis=0, keepdims=True)

    target = jnp.where(valid, target, targets)
    key = target * SLOTS + across[:1]
    key_down, target_down = upright(key), upright(target)
    source_down = upright(jnp.where(valid, source, 0))
    rank = jnp.sum(jnp.where(key < key_down, 1, 0), axis=1, keepdims=True)
    here = rank == across
    one = jnp.ones_like(rank)
    same = pick(target_down + 1, here) == pick(target_down + 1, rank + 1 == across)
    upto = pick(one, key_down < (across + 1) * SLOTS)
    some = pick(one, target_down == across)
    last = jnp.where(some > 0, upto - 1, SLOTS)
    return (pick(down[:, :1], here), jnp.where(same, 1, 0), pick(source_down, here), last)


def factor(m_ref):
    rest = m_ref[...]
    done = []
    for b in range(8):
        shape = rest.shape
        row = lax.broadcasted_iota(jnp.int32, shape, 0)
        cols = [jnp.broadcast_to(rest[:, 8 * b + i : 8 * b + i + 1], shape) for i in range(8)]
        for j in range(0, 8, 2):
            c0, c1 = cols[j], cols[j + 1]
            one, off, two = c0[j : j + 1], c0[j + 1 : j + 2], c1[j + 1 : j + 2]
            inv0 = 1.0 / one
            inv1 = one * (1.0 / (one * two - off * off))
            share = off * inv0
            r0 = rest[j : j + 1]
            r1 = rest[j + 1 : j + 2] - share * r0
            c1 = c1 - share * c0
            for i in range(j + 2, 8):
                cols[i] = cols[i] - c0 * (c0[i : i + 1] * inv0) - c1 * (c1[i : i + 1] * inv1)
            low = row > j + 1
            new = rest - jnp.where(low, c0, 0.0) * (inv0 * r0) - jnp.where(low, c1, 0.0) * (inv1 * r1)
            rest = jnp.where(row == j + 1, jnp.broadcast_to(r1, shape), new)
        done.append(rest[:8])
        rest = rest[8:]
    mat = jnp.concatenate(done, axis=0)
    lanes = lax.broadcasted_iota(jnp.int32, (64, 128), 1)
    row = lax.broadcasted_iota(jnp.int32, (64, 128), 0)
    diag = jnp.sum(jnp.where(lanes == row, mat, 0.0), axis=1, keepdims=True)
    m_ref[...] = jnp.where((lanes >= 64) | (lanes >= row), mat * lax.rsqrt(diag), 0.0)


def kernel(
    rows_ref, cols_ref, start_hbm, blocks_hbm, basis_ref, alpha_ref, beta_ref,
    start_ref, blocks_ref, plan_ref, table, copy_sem, q_ref, y_ref, r_ref, x_ref, m_ref, sums, held, buffers,
    ar_src, ar1, ar_s1, ar2, ar_s2, ar3, ar_s3, ar4, ar_send, ar_recv,
):
    r = lax.axis_index("row")
    c = lax.axis_index("col")
    z, k = r // 2, lax.rem(r, 2)
    cp, ch = lax.rem(c, 8), c // 8
    sibling = (z * 2 + (1 - k), c)
    mine, other = k * 16, (1 - k) * 16

    def along_z(o):
        there = lax.rem(z + o + NZ, NZ)
        return there, (there * 2 + k, c)

    def along_c(o):
        there = lax.rem(c + o, NC)
        return there, (r, there)

    start_copy = pltpu.make_async_copy(start_hbm, start_ref, copy_sem.at[0])
    start_copy.start()
    blocks_copy = pltpu.make_async_copy(blocks_hbm, blocks_ref, copy_sem.at[1])
    blocks_copy.start()

    barrier = pltpu.get_barrier_semaphore()
    for o in range(1, 16):
        pl.semaphore_signal(barrier, inc=1, device_id=along_z(o)[1], device_id_type=MESH)
        pl.semaphore_signal(barrier, inc=1, device_id=along_c(o)[1], device_id_type=MESH)
    pl.semaphore_signal(barrier, inc=1, device_id=sibling, device_id_type=MESH)
    for o in range(1, 8):
        there = (sibling[0], ch * 8 + lax.rem(cp + o, 8))
        pl.semaphore_signal(barrier, inc=1, device_id=there, device_id_type=MESH)

    def plan(row, i):
        return jnp.clip(table[row, i], 0, {3: SLOTS, 6: NC - 1, 7: SLOTS}.get(row, SLOTS - 1))

    def push(src, dst, send, recv, where):
        pltpu.make_async_remote_copy(
            src_ref=src, dst_ref=dst, send_sem=send, recv_sem=recv, device_id=where, device_id_type=MESH
        ).start()

    def settle(ref, sem):
        pltpu.make_async_copy(ref, ref, sem).wait()

    def reduce_1(s):
        ar_src[s] = x_ref[...].reshape(8, 8, 128)
        ar1[s, c] = ar_src[s, cp]
        for o in range(1, 16):
            there, where = along_c(o)
            push(ar_src.at[s, lax.rem(there, 8)], ar1.at[s, c], ar_send.at[s, 0], ar_recv.at[s, 0], where)

    def reduce_2(s):
        settle(ar1.at[s, pl.ds(0, 15)], ar_recv.at[s, 0])
        total = ar1[s, 0]
        for i in range(1, 16):
            total = total + ar1[s, i]
        ar_s1[s, 0] = total[0:4]
        ar_s1[s, 1] = total[4:8]
        push(ar_s1.at[s, 1 - k], ar2.at[s], ar_send.at[s, 1], ar_recv.at[s, 1], sibling)

    def reduce_3(s):
        settle(ar2.at[s], ar_recv.at[s, 1])
        ar_s2[s] = ar_s1[s, k] + ar2[s]
        ar3[s, z] = ar_s2[s]
        for o in FAR:
            push(ar_s2.at[s], ar3.at[s, z], ar_send.at[s, 2], ar_recv.at[s, 2], along_z(o)[1])

    def reduce_4(s):
        settle(ar3.at[s, pl.ds(0, 15)], ar_recv.at[s, 2])
        total = ar3[s, 0]
        for i in range(1, 16):
            total = total + ar3[s, i]
        ar_s3[s] = total
        ar4[s, cp, k] = total
        for o in range(8):
            there = ch * 8 + lax.rem(cp + o, 8)
            for row in (r, sibling[0]) if o else (sibling[0],):
                push(ar_s3.at[s], ar4.at[s, cp, k], ar_send.at[s, 3], ar_recv.at[s, 3], (row, there))

    def reduce_5(s):
        settle(ar3.at[s, pl.ds(0, 15)], ar_recv.at[s, 3])
        for i in range(8):
            for h in range(2):
                x_ref[8 * i + 4 * h : 8 * i + 4 * h + 4] = ar4[s, i, h] * (1.0 / (512 * 128))

    def reduce_end(s):
        settle(ar1.at[s, pl.ds(0, 15)], ar_send.at[s, 0])
        settle(ar2.at[s], ar_send.at[s, 1])
        settle(ar3.at[s, pl.ds(0, 15)], ar_send.at[s, 2])
        settle(ar3.at[s, pl.ds(0, 15)], ar_send.at[s, 3])

    def spread(t, value):
        u = buffers[t]
        value = value.astype(u["src"].dtype)
        u["src"][...] = value
        u["stripe"][c] = value
        u["colset"][mine] = value
        u["row_dst"][c] = jnp.zeros_like(value)
        for o, slot in ((6, 4), (-6, 3), (3, 2), (-3, 1)):
            sem = u["recv"].at[1 if slot > 2 else 0]
            push(u["src"], u["colset"].at[mine + slot], u["send"].at[0], sem, along_z(o)[1])
        push(u["src"], u["colset"].at[mine + 6], u["send"].at[0], u["recv"].at[2], along_z(1)[1])
        push(u["src"], u["colset"].at[mine + 11], u["send"].at[0], u["recv"].at[2], along_z(-1)[1])
        push(u["src"], u["colset"].at[mine + 5], u["send"].at[0], u["recv"].at[2], along_z(8)[1])
        for o in range(1, 16):
            push(u["src"], u["stripe"].at[c], u["send"].at[3], u["recv"].at[3], along_c(o)[1])

    def hop(t, first):
        u = buffers[t]
        settle(u["colset"].at[pl.ds(0, 2)], u["recv"].at[0 if first == 1 else 1])
        source = u["colset"].at[pl.ds(mine + first, 2)]
        for o, base in ((1, 6), (-1, 11)):
            target = u["colset"].at[pl.ds(mine + base + first, 2)]
            push(source, target, u["send"].at[0], u["recv"].at[2], along_z(o)[1])

    def relay(t, first, count):
        u = buffers[t]
        part = u["colset"].at[pl.ds(mine + first, count)]
        push(part, part, u["send"].at[4], u["recv"].at[4], sibling)

    def products(base, source, transposed):
        dims = (((1,), (1,)), ((), ())) if transposed else (((1,), (0,)), ((), ()))

        def one(p, total):
            value = source[plan(base + 2, p)]
            matrix = blocks_ref[plan(base, p)]
            high = value.astype(BF16)
            part = lax.dot_general(high, matrix, dims, preferred_element_type=F32)
            if value.dtype == F32:
                low = (value - high.astype(F32)).astype(BF16)
                part = part + lax.dot_general(low, matrix, dims, preferred_element_type=F32)
            total = jnp.where(plan(base + 1, p) > 0, total, 0.0) + part
            sums[p] = total
            return total

        lax.fori_loop(0, SLOTS, one, jnp.zeros((64, 128), F32), unroll=8)

    def backward(t):
        u = buffers[t]
        kind = u["src"].dtype
        settle(u["stripe"].at[pl.ds(0, 15)], u["recv"].at[3])
        products(4, u["stripe"], False)
        for i in range(NZ):
            u["pair_src"][i] = sums[plan(7, other + i)].astype(kind)
        push(u["pair_src"], u["pair_dst"], u["send"].at[5], u["recv"].at[5], sibling)
        settle(u["pair_dst"], u["recv"].at[5])
        for i in range(15, 4, -1):
            u["zed_src"][i] = (sums[plan(7, mine + i)] + u["pair_dst"][i].astype(F32)).astype(kind)
            if i == 11:
                push(u["zed_src"].at[pl.ds(11, 5)], u["near"].at[pl.ds(0, 5)], u["send"].at[6], u["recv"].at[6], along_z(1)[1])
            if i == 6:
                push(u["zed_src"].at[pl.ds(6, 5)], u["near"].at[pl.ds(5, 5)], u["send"].at[6], u["recv"].at[6], along_z(-1)[1])
        push(u["zed_src"].at[5], u["far"].at[4], u["send"].at[7], u["recv"].at[7], along_z(8)[1])
        for i in range(5):
            held[i] = sums[plan(7, mine + i)] + u["pair_dst"][i].astype(F32)

    def forward(t):
        u = buffers[t]
        settle(u["colset"].at[pl.ds(0, 16)], u["recv"].at[4])
        products(0, u["colset"], True)
        for o in range(1, 16):
            there, where = along_c(o)
            u["row_src"][there] = sums[plan(3, there)].astype(u["src"].dtype)
            push(u["row_src"].at[there], u["row_dst"].at[c], u["send"].at[8], u["recv"].at[8], where)

    def pass_on(t):
        u = buffers[t]
        settle(u["near"], u["recv"].at[6])
        for i, o in ((3, 6), (4, -6), (1, 3), (2, -3)):
            total = held[i] + u["near"][i].astype(F32) + u["near"][5 + i].astype(F32)
            u["zed_src"][i] = total.astype(u["src"].dtype)
            push(u["zed_src"].at[i], u["far"].at[i - 1], u["send"].at[7], u["recv"].at[7], along_z(o)[1])

    def collect(t):
        u = buffers[t]
        total = held[0] + u["near"][0].astype(F32) + u["near"][5].astype(F32) + sums[plan(3, c)]
        settle(u["row_dst"].at[pl.ds(0, 15)], u["recv"].at[8])
        for i in range(NC):
            total = total + u["row_dst"][i].astype(F32)
        settle(u["far"], u["recv"].at[7])
        for i in range(5):
            total = total + u["far"][i].astype(F32)
        return total

    def operator_end(t):
        u = buffers[t]
        settle(u["colset"].at[pl.ds(0, 15)], u["send"].at[0])
        settle(u["stripe"].at[pl.ds(0, 15)], u["send"].at[3])
        settle(u["colset"].at[pl.ds(0, 16)], u["send"].at[4])
        settle(u["pair_dst"], u["send"].at[5])
        settle(u["near"], u["send"].at[6])
        settle(u["far"], u["send"].at[7])
        settle(u["row_dst"].at[pl.ds(0, 15)], u["send"].at[8])

    lanes = lax.broadcasted_iota(jnp.int32, (64, 64), 1)
    rows = lax.broadcasted_iota(jnp.int32, (64, 64), 0)
    eye = (lanes == rows).astype(F32)

    def factor_start():
        m_ref[:, 0:64] = x_ref[:, 0:64]
        m_ref[:, 64:128] = eye
        factor(m_ref)

    def factor_step(t):
        alpha_t = x_ref[:, 64:128]
        alpha_ref[t] = alpha_t
        m_ref[:, 0:64] = x_ref[:, 0:64] - nt(alpha_t, alpha_t)
        m_ref[:, 64:128] = eye
        factor(m_ref)
        beta_ref[t] = m_ref[:, 0:64]
        return alpha_t

    sums[SLOTS] = jnp.zeros((64, 128), F32)
    plan_ref[...] = jnp.zeros((8, 128), jnp.int32)
    row_index, col_index = rows_ref[...], cols_ref[...]
    valid = row_index < 512
    owner = lax.shift_right_logical(col_index, 4)
    away = (lax.shift_right_logical(owner, 1) - z + NZ) & 15
    slot = jnp.zeros_like(away)
    for i in range(1, NZ):
        slot = jnp.where(away == REACH[i], i, slot)
    row_target = jnp.clip(row_index - r * NC, 0, NC - 1)
    col_target = (owner & 1) * NZ + slot
    for base, part in (
        (0, plan_part(row_target, col_target, valid, SLOTS)),
        (4, plan_part(col_target, row_target, valid, SLOTS)),
    ):
        for i in range(4):
            plan_ref[base + i : base + i + 1, 0:SLOTS] = part[i]
    plan_copy = pltpu.make_async_copy(plan_ref, table, copy_sem.at[2])
    plan_copy.start()
    start_copy.wait()
    first = start_ref[...]
    x_ref[...] = nt(first, jnp.concatenate([first, first], axis=0))
    blocks_copy.wait()
    plan_copy.wait()
    pl.semaphore_wait(barrier, 38)

    for s in range(ITERS):
        if s:
            x_ref[...] = nt(r_ref[...], jnp.concatenate([r_ref[...], q_ref[...]], axis=0))
        if s == 0:
            spread(s, first)
        reduce_1(s)
        if s:
            spread(s, r_ref[...])
        hop(s, 1)
        reduce_2(s)
        hop(s, 3)
        relay(s, 0, 5)
        reduce_3(s)
        backward(s)
        settle(buffers[s]["colset"].at[pl.ds(0, 11)], buffers[s]["recv"].at[2])
        relay(s, 5, 11)
        forward(s)
        pass_on(s)
        reduce_4(s)
        reduce_5(s)
        if s == 0:
            factor_start()
            inverse = m_ref[:, 64:128]
            q_ref[...] = nn(inverse, first)
            y_ref[...] = nn(inverse, collect(s))
            r_ref[...] = y_ref[...]
        else:
            alpha_t = factor_step(s - 1)
            inverse = m_ref[:, 64:128]
            following = nn(inverse, r_ref[...] - nn(alpha_t, q_ref[...]))
            less = nn(alpha_t, y_ref[...])
            carried = nn(m_ref[:, 0:64], q_ref[...])
            y_ref[...] = nn(inverse, collect(s) - less)
            r_ref[...] = y_ref[...] - carried
            q_ref[...] = following
    x_ref[...] = nt(r_ref[...], jnp.concatenate([r_ref[...], q_ref[...]], axis=0))
    reduce_1(ITERS)
    for s in range(ITERS):
        operator_end(s)
        reduce_end(s)
    reduce_2(ITERS)
    reduce_3(ITERS)
    reduce_4(ITERS)
    reduce_5(ITERS)
    alpha_t = factor_step(ITERS - 1)
    basis_ref[...] = nn(m_ref[:, 64:128], r_ref[...] - nn(alpha_t, q_ref[...]))
    reduce_end(ITERS)


def finish(basis_ref, alpha_ref, beta_ref, basis_out, alpha_out, beta_out):
    basis_out[...] = basis_ref[...]
    for t in range(ITERS):
        alpha_out[t] = alpha_ref[t].T
        beta_out[t] = beta_ref[t].T


def shards(blocks, block_rows, block_cols, start):
    vmem = pl.BlockSpec(memory_space=pltpu.VMEM)
    shapes = (
        jax.ShapeDtypeStruct((64, 128), F32),
        jax.ShapeDtypeStruct((ITERS, 64, 64), F32),
        jax.ShapeDtypeStruct((ITERS, 64, 64), F32),
    )
    half = (ITERS + 1, 4, 128)

    def buffer(kind):
        counts = dict(
            stripe=16, colset=32, pair_src=16, pair_dst=16, zed_src=16, near=10, far=5, row_src=16, row_dst=16
        )
        made = {name: pltpu.VMEM((count, 64, 128), kind) for name, count in counts.items()}
        made["src"] = pltpu.VMEM((64, 128), kind)
        made["send"] = pltpu.SemaphoreType.DMA((9,))
        made["recv"] = pltpu.SemaphoreType.DMA((9,))
        return made

    basis, alphas, betas = pl.pallas_call(
        kernel,
        out_shape=shapes,
        in_specs=[vmem, vmem, HBM, HBM],
        out_specs=(vmem, vmem, vmem),
        scratch_shapes=[
            pltpu.VMEM((64, 128), F32),
            pltpu.VMEM((SLOTS, 128, 128), BF16),
            pltpu.VMEM((8, 128), jnp.int32),
            pltpu.SMEM((8, 128), jnp.int32),
            pltpu.SemaphoreType.DMA((3,)),
            pltpu.VMEM((64, 128), F32),
            pltpu.VMEM((64, 128), F32),
            pltpu.VMEM((64, 128), F32),
            pltpu.VMEM((64, 128), F32),
            pltpu.VMEM((64, 128), F32),
            pltpu.VMEM((SLOTS + 1, 64, 128), F32),
            pltpu.VMEM((5, 64, 128), F32),
            [buffer(F32), buffer(BF16), buffer(BF16)],
            pltpu.VMEM((ITERS + 1, 8, 8, 128), F32),
            pltpu.VMEM((ITERS + 1, 16, 8, 128), F32),
            pltpu.VMEM((ITERS + 1, 2, 4, 128), F32),
            pltpu.VMEM(half, F32),
            pltpu.VMEM(half, F32),
            pltpu.VMEM((ITERS + 1, 16, 4, 128), F32),
            pltpu.VMEM(half, F32),
            pltpu.VMEM((ITERS + 1, 8, 2, 4, 128), F32),
            pltpu.SemaphoreType.DMA((ITERS + 1, 4)),
            pltpu.SemaphoreType.DMA((ITERS + 1, 4)),
        ],
        compiler_params=pltpu.CompilerParams(collective_id=0, has_side_effects=True, vmem_limit_bytes=60 << 20),
        name="lanczos",
    )(block_rows.reshape(1, SLOTS), block_cols.reshape(1, SLOTS), start, blocks)
    return pl.pallas_call(
        finish,
        out_shape=shapes,
        in_specs=[vmem] * 3,
        out_specs=(vmem,) * 3,
        name="finish",
    )(basis, alphas, betas)


def solution(mesh):
    in_specs = (
        P(("row", "col"), None, None),
        P(("row", "col")),
        P(("row", "col")),
        P(None, ("row", "col")),
    )
    out_specs = (P(None, ("row", "col")), P(), P())
    return jax.shard_map(shards, mesh=mesh, in_specs=in_specs, out_specs=out_specs, check_vma=False)
```
